32 devices in a mesh: groups: 2 (over y), gx: 4 (over x, core), gy: 4 (over z).
Axes of the slice: x: 2, y: 2, z: 4, core: 2. Of those that a mesh axis runs over, the one named last changes fastest.
Arguments:
- tokens: bfloat16 [2048, 16384], P(('groups', 'gy'), 'gx'), parts along dimension 0, may hold values from -1000 to 1000
- norm_gain: float32 [16384], P('gx'), may hold values from 0.1 to 1.9
- qkv_weight: bfloat16 [16384, 18432], P('gx', 'gy'), may hold values from -0.046875 to 0.046875
- out_weight: bfloat16 [16384, 16384], P('gy', 'gx'), may hold values from -1.5 to 1.5
- key_cache: bfloat16 [4, 3072, 1024], P('groups', None, 'gy'), parts along dimension 0, may hold values from -400 to 400
- value_cache: bfloat16 [4, 3072, 1024], P('groups', None, 'gy'), parts along dimension 0, may hold values from -6 to 6
- prefix_len: int32 [4], P('groups'), parts along dimension 0, may hold values from 512 to 3072, as said below
- stretch_len: int32 [4], P('groups'), parts along dimension 0, may hold values from 128 to 512, as said below
Outputs:
- block_output: bfloat16 [2048, 16384], P(('groups', 'gy'), 'gx'), parts along dimension 0
The draws below stay inside these ranges and needn't reach their ends.
There are 2 independent parts, one for each index of `groups`. The reference program is written for one: setup_inputs(seed, part) draws one part's arguments, and reference() takes and returns one part's arrays. A program takes and returns all parts, laid end to end along the dimension named above; an argument that names none is the same for every part. Nothing has to cross between parts.
Inputs may be any that keep to these rules, and one draw needn't show every extreme that they name: `prefix_len`: one request in every draw has exactly 3072 cached positions. `stretch_len`: one request in every draw has all 512 tokens live.
All inputs are finite; a program needn't handle non-finite values.
Results may differ from the reference program's by a relative error of at most 0.012.
The reference program's roundings to bfloat16 on the way (of `normed`, `probs` and `attended`) count: a program that leaves them out, or rounds other values in their place, can miss the bound.
Values may be sent and summed in bfloat16 or wider, within the bound.
No kernel may reach another device: no remote copies, remote signals or barrier semaphores. Data moves between devices by JAX's collectives and lax.ppermute only.
A program may use at most 448 MiB of HBM per device.

```python
import math
import jax
import jax.numpy as jnp
from jax import lax

D = 16384
QH = 128
KVH = 8
HD = 128
STRETCH = 512
REQS = 2
PREFIX = 3072
G = 16
TOKENS = 1024


def draw_tokens(key, part):
    key = jax.random.fold_in(key, 11)
    first, second, third = jax.random.split(key, 3)
    ramp = jnp.exp(math.log(3.0) * jnp.arange(D, dtype=jnp.float32) / D)
    columns = ramp * jnp.exp(math.log(2.0) * jax.random.uniform(third, (D,), jnp.float32))
    base = jnp.clip(jax.random.normal(first, (TOKENS, D), jnp.float32), -6.0, 6.0)
    scales = jnp.exp(math.log(10.0) * jax.random.uniform(second, (TOKENS, 1), jnp.float32))
    return (base * scales * columns[None, :]).astype(jnp.bfloat16)


def draw_key_cache(key, part):
    key = jax.random.fold_in(key, 23)
    first = jax.random.fold_in(key, 0)
    base = jnp.clip(jax.random.normal(first, (REQS, PREFIX, KVH * HD), jnp.float32), -6.0, 6.0)
    return base.astype(jnp.bfloat16)


def draw_prefix_len(key, part):
    key = jax.random.fold_in(key, 37)
    first, second = jax.random.split(key)
    values = jax.random.randint(first, (REQS,), STRETCH, PREFIX + 1, jnp.int32)
    chosen = jax.random.randint(second, (), 0, REQS, jnp.int32)
    return jnp.where(jnp.arange(REQS, dtype=jnp.int32) == chosen, PREFIX, values).astype(jnp.int32)


def draw_stretch_len(key, part):
    key = jax.random.fold_in(key, 41)
    first, second = jax.random.split(key)
    values = jax.random.randint(first, (REQS,), STRETCH // 4, STRETCH + 1, jnp.int32)
    chosen = jax.random.randint(second, (), 0, REQS, jnp.int32)
    return jnp.where(jnp.arange(REQS, dtype=jnp.int32) == chosen, STRETCH, values).astype(jnp.int32)


def steps_of(rng, extent, shards, least, top_value):
    loudness = 1.0
    for axis_at, parts in shards:
        heights = jax.random.uniform(jax.random.fold_in(jax.random.fold_in(rng, 6), axis_at), (parts,), jnp.float32, least / len(shards), top_value / len(shards))
        loudness = loudness * jnp.repeat(jnp.exp(heights), extent[axis_at] // parts).reshape((-1,) + (1,) * (len(extent) - 1 - axis_at))
    return loudness


def noise(stream_key, shape, scale, limit, cuts=(), kind=jnp.bfloat16):
    loudness = steps_of(stream_key, shape, cuts, -0.22, 0.18) if cuts else 1.0
    entries = jax.random.normal(stream_key, shape, jnp.float32) * scale * loudness
    return jnp.minimum(jnp.maximum(entries, -limit), limit).astype(kind)


def setup_inputs(seed: int = 0, part: int = 0) -> dict:
    key_list = jax.random.split(jax.random.key(seed), 9)
    own_keys = jax.random.split(jax.random.fold_in(key_list[8], part), 9)
    tokens = draw_tokens(jax.random.fold_in(jax.random.fold_in(key_list[8], part), 71), part)
    norm_gain = jnp.clip(1.0 + 0.18 * jax.random.normal(key_list[1], (D,), jnp.float32), 0.1, 1.9)
    qkv_weight = noise(key_list[2], (D, KVH * (G + 2) * HD), D ** -0.5, 0.046875, ((0, 4), (1, 4)))
    out_weight = noise(key_list[3], (QH * HD, D), (QH * HD // 1024) ** -0.5, 1.5, ((0, 4), (1, 4)))
    key_cache = draw_key_cache(jax.random.fold_in(jax.random.fold_in(key_list[8], part), 71), part)
    value_cache = noise(own_keys[5], (REQS, PREFIX, KVH * HD), 1.0, 6.0, ((2, 4),))
    prefix_len = draw_prefix_len(jax.random.fold_in(jax.random.fold_in(key_list[8], part), 71), part)
    stretch_len = draw_stretch_len(jax.random.fold_in(jax.random.fold_in(key_list[8], part), 71), part)
    return {"tokens": tokens, "norm_gain": norm_gain, "qkv_weight": qkv_weight, "out_weight": out_weight, "key_cache": key_cache, "value_cache": value_cache, "prefix_len": prefix_len, "stretch_len": stretch_len}


THETA = 500000.0
EPSILON = 1e-05

def rotate(values, positions):
    half = values.shape[-1] // 2
    freq = THETA ** (-(jnp.arange(half, dtype=jnp.float32) * 2.0) / values.shape[-1])
    angles = positions.astype(jnp.float32)[:, None] * freq[None, :]
    cosine = jnp.concatenate([jnp.cos(angles), jnp.cos(angles)], -1)[:, None, :]
    sine = jnp.concatenate([jnp.sin(angles), jnp.sin(angles)], -1)[:, None, :]
    turned = jnp.concatenate([-values[..., half:], values[..., :half]], -1)
    return values * cosine + turned * sine

def row_positions(row_ids, prefix_len):
    request = row_ids // STRETCH
    match = request[:, None] == jnp.arange(prefix_len.shape[0], dtype=jnp.int32)[None, :]
    start = lax.optimization_barrier(jnp.sum(jnp.where(match, prefix_len[None, :], 0), axis=1))
    return (start + row_ids % STRETCH).astype(jnp.int32)

def attend(queries, offsets, cached_keys, cached_values, fresh_keys, fresh_values, prefix, live):
    keys = jnp.concatenate([cached_keys, fresh_keys], 0)
    values = jnp.concatenate([cached_values, fresh_values], 0)
    scores = jnp.dot(queries, keys.T, preferred_element_type=jnp.float32) * queries.shape[-1] ** (-0.5)
    span = cached_keys.shape[0]
    places = jnp.arange(keys.shape[0], dtype=jnp.int32)
    shifted = places - span
    allowed = jnp.where((places < span)[None, :], (places < prefix)[None, :], (shifted[None, :] < live) & (shifted[None, :] <= offsets[:, None]))
    scores = jnp.where(allowed, scores, -1e+30)
    highest = lax.optimization_barrier(jnp.max(scores, axis=1, keepdims=True))
    weights = jnp.where(allowed, jnp.exp(scores - highest), 0.0)
    total = lax.optimization_barrier(jnp.sum(weights, axis=1, keepdims=True))
    probs = (weights / total).astype(jnp.bfloat16)
    return jnp.dot(probs, values, preferred_element_type=jnp.float32).astype(jnp.bfloat16)

def reference(tokens, norm_gain, qkv_weight, out_weight, key_cache, value_cache, prefix_len, stretch_len):
    widened = tokens.astype(jnp.float32)
    meansq = lax.optimization_barrier(jnp.sum(widened * widened, axis=1)) / D
    normed = (widened * lax.rsqrt(meansq + EPSILON)[:, None] * norm_gain[None, :]).astype(jnp.bfloat16)
    projected = jnp.dot(normed, qkv_weight, preferred_element_type=jnp.float32)
    group = QH // KVH
    blocks = projected.reshape(TOKENS, KVH, group + 2, HD)
    positions = row_positions(jnp.arange(TOKENS, dtype=jnp.int32), prefix_len)
    queries = rotate(blocks[:, :, :group].reshape(TOKENS, KVH * group, HD), positions)
    queries = queries.astype(jnp.bfloat16).reshape(TOKENS, KVH, group, HD)
    fresh_keys = rotate(blocks[:, :, group], positions).astype(jnp.bfloat16)
    fresh_values = blocks[:, :, group + 1].astype(jnp.bfloat16)
    offsets = jnp.tile(jnp.arange(STRETCH, dtype=jnp.int32), group)
    request_rows = []
    for request in range(REQS):
        lower = request * STRETCH
        upper = lower + STRETCH
        head_blocks = []
        for head_group in range(KVH):
            stacked = queries[lower:upper, head_group].transpose(1, 0, 2).reshape(group * STRETCH, HD)
            result = attend(stacked, offsets, key_cache[request, :, head_group * HD:(head_group + 1) * HD], value_cache[request, :, head_group * HD:(head_group + 1) * HD], fresh_keys[lower:upper, head_group], fresh_values[lower:upper, head_group], prefix_len[request], stretch_len[request])
            head_blocks.append(result.reshape(group, STRETCH, HD).transpose(1, 0, 2).reshape(STRETCH, group * HD))
        request_rows.append(jnp.concatenate(head_blocks, 1))
    attended = jnp.concatenate(request_rows, 0)
    return jnp.dot(attended, out_weight, preferred_element_type=jnp.float32).astype(jnp.bfloat16)
```

```python
import math

import jax
import jax.numpy as jnp
from jax import lax
from jax.experimental import pallas as pl
from jax.experimental.pallas import tpu as pltpu
from jax.sharding import PartitionSpec as P

D = 16384
QH = 128
KVH = 8
HD = 128
STRETCH = 512
G = QH // KVH

THETA = 500000.0
EPSILON = 1e-05
QSCALE = HD ** (-0.5) * math.log2(math.e)

F32 = jnp.float32
BF16 = jnp.bfloat16
TILE = 256
VMEM_LIMIT = 56 * 1024 * 1024


HINT = pl.CostEstimate(flops=1024, bytes_accessed=1024, transcendentals=0)

LONGER = pl.CostEstimate(flops=1024, bytes_accessed=2**25, transcendentals=0)


def params(**kw):
    return pltpu.CompilerParams(vmem_limit_bytes=VMEM_LIMIT, **kw)


def sds(shape, dtype):
    return jax.ShapeDtypeStruct(shape, dtype)


def whole(*_):
    return (0, 0)


PER = 2


def project_kernel(s_ref, *refs, sources):
    x_refs, refs = refs[:sources], refs[sources:]
    w_refs, (*peer_refs, own_ref, x_ref, sem) = refs[:PER], refs[PER:]
    step = pl.program_id(0)
    half = x_refs[0].shape[0]

    def fetch(pair):
        for i, ref in enumerate(pair):
            pltpu.make_async_copy(ref, x_ref.at[pl.ds(i * half, half)], sem.at[i]).start()
        for i, ref in enumerate(pair):
            pltpu.make_async_copy(ref, x_ref.at[pl.ds(i * half, half)], sem.at[i]).wait()

    @pl.when(step == 0)
    def _():
        if sources == 2:
            fetch(x_refs)
        else:

            @pl.when(s_ref[0] == 1)
            def _():
                fetch(x_refs[:2])

            @pl.when(s_ref[0] == 0)
            def _():
                fetch(x_refs[2:])

    peer_steps = 10 // PER
    products = [jnp.dot(x_ref[...], w[...], preferred_element_type=F32) for w in w_refs]

    @pl.when(step < peer_steps)
    def _():
        for v, o_ref in zip(products, peer_refs):
            o_ref[...] = v.astype(BF16)

    @pl.when(step >= peer_steps)
    def _():
        for i, v in enumerate(products):
            own_ref[:, i * TILE : (i + 1) * TILE] = v


def project(info, xs, w):
    half, depth = xs[0].shape
    peer_steps = 10 // PER
    steps = 18 // PER
    weights = [
        pl.BlockSpec((depth, TILE), lambda j, s, i=i: (0, s[1 + j * PER + i])) for i in range(PER)
    ]
    rows = 2 * half
    return pl.pallas_call(
        lambda *refs: project_kernel(*refs, sources=len(xs)),
        grid_spec=pltpu.PrefetchScalarGridSpec(
            num_scalar_prefetch=1,
            grid=(steps,),
            in_specs=[pl.BlockSpec(memory_space=pl.ANY)] * len(xs) + weights,
            out_specs=[
                pl.BlockSpec((rows, TILE), lambda j, s: (0, jnp.minimum(j, peer_steps - 1))),
                pl.BlockSpec((rows, TILE), lambda j, s: (0, jnp.minimum(j, peer_steps - 1))),
                pl.BlockSpec((rows, PER * TILE), lambda j, s: (0, jnp.maximum(j - peer_steps, 0))),
            ],
            scratch_shapes=[pltpu.VMEM((rows, depth), BF16), pltpu.SemaphoreType.DMA((2,))],
        ),
        out_shape=[sds((rows, 5 * TILE), BF16)] * 2 + [sds((rows, 8 * TILE), F32)],
        compiler_params=params(),
        cost_estimate=HINT,
        name="project",
    )(info, *xs, *([w] * PER))


def core_sums(s_ref, own_ref, kv_refs, recv_refs):
    n = recv_refs[0].shape[1]
    first = s_ref[0] == 0
    mine = jnp.where(first, kv_refs[0][...].astype(F32), kv_refs[1][...].astype(F32))
    theirs = jnp.where(first, kv_refs[2][...].astype(F32), kv_refs[3][...].astype(F32))
    halves = [
        own_ref[:, i * n : (i + 1) * n] + r[...].astype(F32) for i, r in enumerate(recv_refs)
    ]
    return halves, mine + theirs


def combine_kernel(s_ref, own_ref, kva_ref, kvb_ref, ra_ref, rb_ref, rka_ref, rkb_ref, o_ref):
    halves, kv = core_sums(s_ref, own_ref, (kva_ref, kvb_ref, rka_ref, rkb_ref), (ra_ref, rb_ref))
    n = ra_ref.shape[1]
    for i, v in enumerate(halves):
        o_ref[:, i * n : (i + 1) * n] = v.astype(BF16)
    o_ref[:, 2 * n :] = kv.astype(BF16)


def sums_specs(rows, n):
    kv = pl.BlockSpec((rows, TILE), lambda i, s: (i, 4))
    half = pl.BlockSpec((rows, n // 2), lambda i, s: (i, s[0]))
    return [pl.BlockSpec((rows, n), lambda i, s: (i, s[0])), kv, kv, half, half, kv, kv]


def combine(chip, own, mine, recv):
    rows = own.shape[0]
    n = own.shape[1] // 2
    part = rows // 2
    other = jnp.reshape(1 - chip, (1,)).astype(jnp.int32)
    return pl.pallas_call(
        combine_kernel,
        grid_spec=pltpu.PrefetchScalarGridSpec(
            num_scalar_prefetch=1,
            grid=(rows // part,),
            in_specs=sums_specs(part, n),
            out_specs=pl.BlockSpec((part, n + TILE), lambda i, s: (i, 0)),
        ),
        out_shape=sds((rows, n + TILE), BF16),
        compiler_params=params(),
        cost_estimate=HINT,
        name="combine",
    )(other, own, *mine, *recv, *recv)


def finish_kernel(s_ref, own_ref, kva_ref, kvb_ref, ra_ref, rb_ref, rka_ref, rkb_ref, *rest):
    x_ref, cos_ref, sin_ref, q_ref, k_ref, v_ref = rest
    halves, kv = core_sums(s_ref, own_ref, (kva_ref, kvb_ref, rka_ref, rkb_ref), (ra_ref, rb_ref))
    n = ra_ref.shape[1]
    cos, sin = cos_ref[...], sin_ref[...]

    def turn(v):
        return v * cos + pltpu.roll(v, HD // 2, 1) * sin

    for i, half in enumerate(halves):
        v = half + x_ref[:, i * n : (i + 1) * n].astype(F32)
        for h in range(n // HD):
            at = i * (n // HD) + h
            q_ref[at] = (turn(v[:, h * HD : (h + 1) * HD]) * QSCALE).astype(BF16)
    kv += x_ref[:, 2 * n :].astype(F32)
    k_ref[...] = turn(kv[:, :HD]).astype(BF16)
    v_ref[...] = kv[:, HD:].astype(BF16)


def finish(chip, own, mine, recv, cross, cos, sin, slot):
    rows = own.shape[0]
    n = own.shape[1] // 2
    part = rows // 2
    here = jnp.reshape(chip, (1,)).astype(jnp.int32)
    row = lambda i, s: (i, 0)
    table = lambda i, s: (slot * (rows // part) + i, 0)
    return pl.pallas_call(
        finish_kernel,
        grid_spec=pltpu.PrefetchScalarGridSpec(
            num_scalar_prefetch=1,
            grid=(rows // part,),
            in_specs=sums_specs(part, n)
            + [
                pl.BlockSpec((part, n + TILE), row),
                pl.BlockSpec((part, HD), table),
                pl.BlockSpec((part, HD), table),
            ],
            out_specs=[
                pl.BlockSpec((n // HD, part, HD), lambda i, s: (0, i, 0)),
                pl.BlockSpec((part, HD), row),
                pl.BlockSpec((part, HD), row),
            ],
        ),
        out_shape=[sds((n // HD, rows, HD), BF16), sds((rows, HD), BF16), sds((rows, HD), BF16)],
        compiler_params=params(),
        cost_estimate=HINT,
        name="finish",
    )(here, own, *mine, *recv, *recv, cross, cos, sin)


KB = 512
CHUNK = 1024
PIECE = 512
LARGE = 2.0**100


def attend_kernel(
    s_ref, q_ref, k_ref, v_ref, ka_ref, kb_ref, va_ref, vb_ref, o_ref, vx_ref, acc_ref, top_ref
):
    prefix, live, half = s_ref[2], s_ref[3], s_ref[4]
    rows = ka_ref.shape[0]
    m_rows = q_ref.shape[0]
    span = k_ref.shape[1]
    fresh = 2 * rows
    vx_ref[:span, :HD] = v_ref[0]
    vx_ref[span : span + rows, :HD] = va_ref[...]
    vx_ref[span + rows :, :HD] = vb_ref[...]
    vx_ref[:, HD:] = jnp.ones((span + fresh, HD), BF16)
    nt = (((1,), (1,)), ((), ()))
    count = prefix // KB
    rest = prefix - count * KB

    def product(a, b):
        return lax.dot_general(a, b, nt, preferred_element_type=F32)

    def scores(cut, at):
        return product(q_ref[cut, :], k_ref[0, pl.ds(at, KB), :])

    def fresh_scores(cut):
        row = lax.broadcasted_iota(jnp.int32, (rows, fresh), 0) + half * rows
        place = lax.broadcasted_iota(jnp.int32, (rows, fresh), 1)
        ok = (place <= row) & (place < live)
        q = q_ref[cut, :]
        s = jnp.concatenate([product(q, ka_ref[...]), product(q, kb_ref[...])], 1)
        s = s.reshape(PIECE // rows, rows, fresh)
        return jnp.where(ok[None], s, -1e30).reshape(PIECE, fresh)

    def rest_scores(cut, at):
        place = lax.broadcasted_iota(jnp.int32, (PIECE, KB), 1)
        return jnp.where(place < rest, scores(cut, at), -1e30)

    def add(s, cut, at):
        p = jnp.exp2(s - top_ref[cut, :1]).astype(BF16)
        acc_ref[cut, :] += jnp.dot(p, vx_ref[pl.ds(at, KB), :], preferred_element_type=F32)

    def raise_top(s, cut):
        top_ref[cut, :] = jnp.maximum(top_ref[cut, :], jnp.max(s, axis=1, keepdims=True))

    def block(i):
        return pl.multiple_of(i * KB, KB)

    def cuts(size, visit):
        def step(i, carry):
            visit(pl.ds(pl.multiple_of(i * size, size), size))
            return carry

        lax.fori_loop(0, m_rows // size, step, 0)

    def blocks(stop, visit):
        def step(i, carry):
            visit(block(i))
            return carry

        lax.fori_loop(0, stop, step, 0)

    def sweep():
        acc_ref[...] = jnp.zeros_like(acc_ref)
        cuts(PIECE, lambda cut: add(fresh_scores(cut), cut, span))

        @pl.when(rest > 0)
        def _():
            at = block(count)
            cuts(PIECE, lambda cut: add(rest_scores(cut, at), cut, at))

        cuts(CHUNK, lambda cut: blocks(count, lambda at: add(scores(cut, at), cut, at)))

    top_ref[...] = jnp.full(top_ref.shape, -1e30, F32)
    cuts(PIECE, lambda cut: raise_top(scores(cut, 0), cut))

    def attempt(i):
        @pl.when(i > 0)
        def _():
            cuts(PIECE, lambda cut: raise_top(fresh_scores(cut), cut))
            cuts(PIECE, lambda cut: blocks(count, lambda at: raise_top(scores(cut, at), cut)))

            @pl.when(rest > 0)
            def _():
                at = block(count)
                cuts(PIECE, lambda cut: raise_top(rest_scores(cut, at), cut))

        sweep()
        return jnp.max(jnp.where(acc_ref[:, HD:] < LARGE, 0.0, 1.0))

    def more(state):
        return (state[0] == 0) | ((state[0] == 1) & (state[1] > 0.0))

    lax.while_loop(more, lambda state: (state[0] + 1, attempt(state[0])), (0, 0.0))

    for h in range(m_rows // rows):
        cut = slice(h * rows, (h + 1) * rows)
        o_ref[:, h * HD : (h + 1) * HD] = (acc_ref[cut, :HD] / acc_ref[cut, HD:]).astype(BF16)


def attend(info, q, key_cache, value_cache, ka, kb, va, vb):
    heads, rows, _ = q.shape
    span = key_cache.shape[1]
    m_rows = heads * rows
    q = q.reshape(m_rows, HD)
    cache = pl.BlockSpec((1, span, HD), lambda i, s: (s[0], 0, s[1]))
    fresh = pl.BlockSpec((rows, HD), whole)
    return pl.pallas_call(
        attend_kernel,
        grid_spec=pltpu.PrefetchScalarGridSpec(
            num_scalar_prefetch=1,
            grid=(1,),
            in_specs=[
                pl.BlockSpec((m_rows, HD), whole),
                cache,
                cache,
                fresh,
                fresh,
                fresh,
                fresh,
            ],
            out_specs=pl.BlockSpec((rows, heads * HD), whole),
            scratch_shapes=[
                pltpu.VMEM((span + 2 * rows, 2 * HD), BF16),
                pltpu.VMEM((m_rows, 2 * HD), F32),
                pltpu.VMEM((m_rows, HD), F32),
            ],
        ),
        out_shape=sds((rows, heads * HD), BF16),
        compiler_params=params(),
        cost_estimate=HINT,
        name="attend",
    )(info, q, key_cache, value_cache, ka, kb, va, vb)


def out_kernel(s_ref, *refs, sources, before, outs):
    a_refs, refs = refs[:sources], refs[sources:]
    x_ref, sem = refs[-2:]
    o_refs = refs[-2 - outs : -2]
    depth = a_refs[0].shape[1]

    @pl.when(pl.program_id(0) == 0)
    def _():
        copies = [
            pltpu.make_async_copy(
                ref, x_ref.at[:, pl.ds(pl.multiple_of(s_ref[i] * depth, depth), depth)], sem.at[i]
            )
            for i, ref in enumerate(a_refs)
        ]
        for c in copies:
            c.start()
        for c in copies:
            c.wait()

    total = jnp.dot(x_ref[...], refs[0][...], preferred_element_type=F32)
    if before:
        total += refs[1][...]
    for i, o_ref in enumerate(o_refs):

        @pl.when(pl.program_id(0) * outs // pl.num_programs(0) == i)
        def _():
            o_ref[...] = total.astype(o_ref.dtype)


def out_project(index, pieces, w, before, first, width, dtype, outs=1, cols=1024):
    rows, depth = pieces[0].shape
    n = len(pieces)
    start = first // cols
    cols = min(cols, width)
    specs = [pl.BlockSpec(memory_space=pl.ANY)] * n + [
        pl.BlockSpec((n * depth, cols), lambda j, s: (s[n], start + j))
    ]
    operands = list(pieces) + [w]
    if before is not None:
        operands.append(before)
        specs.append(pl.BlockSpec((rows, cols), lambda j, s: (0, start + j)))
    each = width // cols // outs
    out = pl.pallas_call(
        lambda *refs: out_kernel(*refs, sources=n, before=before is not None, outs=outs),
        grid_spec=pltpu.PrefetchScalarGridSpec(
            num_scalar_prefetch=1,
            grid=(width // cols,),
            in_specs=specs,
            out_specs=[
                pl.BlockSpec((rows, cols), lambda j, s, i=i: (0, jnp.clip(j - i * each, 0, each - 1)))
                for i in range(outs)
            ],
            scratch_shapes=[pltpu.VMEM((rows, n * depth), BF16), pltpu.SemaphoreType.DMA((n,))],
        ),
        out_shape=[sds((rows, width // outs), dtype)] * outs,
        compiler_params=params(),
        cost_estimate=HINT,
        name="out_project",
    )(index, *operands)
    return out[0] if outs == 1 else out


def choose_kernel(s_ref, a_ref, b_ref, o_ref):
    o_ref[...] = jnp.where(s_ref[0] == 1, a_ref[...], b_ref[...])


def choose(flag, a, b):
    rows, cols = a.shape
    part = rows // 2
    block = pl.BlockSpec((part, cols), lambda i, s: (i, 0))
    return pl.pallas_call(
        choose_kernel,
        grid_spec=pltpu.PrefetchScalarGridSpec(
            num_scalar_prefetch=1,
            grid=(rows // part,),
            in_specs=[block] * 2,
            out_specs=block,
        ),
        out_shape=sds(a.shape, a.dtype),
        compiler_params=params(),
        cost_estimate=LONGER,
        name="choose",
    )(flag.astype(jnp.int32)[None], a, b)


def add_kernel(*refs):
    total = refs[0][...].astype(F32)
    for ref in refs[1:-1]:
        total += ref[...].astype(F32)
    refs[-1][...] = total.astype(BF16)


def add(*xs):
    rows, cols = xs[0].shape
    block = pl.BlockSpec((rows, cols), lambda: (0, 0))
    return pl.pallas_call(
        add_kernel,
        in_specs=[block] * len(xs),
        out_specs=block,
        out_shape=sds((rows, cols), BF16),
        compiler_params=params(),
        cost_estimate=HINT,
        name="add",
    )(*xs)


def in_turn_kernel(s_ref, ka_ref, kb_ref, va_ref, vb_ref, k0_ref, k1_ref, v0_ref, v1_ref):
    first = s_ref[0] == 1

    @pl.when(first)
    def _():
        k0_ref[...], k1_ref[...] = ka_ref[...], kb_ref[...]
        v0_ref[...], v1_ref[...] = va_ref[...], vb_ref[...]

    @pl.when(jnp.logical_not(first))
    def _():
        k0_ref[...], k1_ref[...] = kb_ref[...], ka_ref[...]
        v0_ref[...], v1_ref[...] = vb_ref[...], va_ref[...]


def in_turn(flag, ka, kb, va, vb):
    block = pl.BlockSpec(ka.shape, whole)
    return pl.pallas_call(
        in_turn_kernel,
        grid_spec=pltpu.PrefetchScalarGridSpec(
            num_scalar_prefetch=1, grid=(1,), in_specs=[block] * 4, out_specs=[block] * 4
        ),
        out_shape=[sds(ka.shape, BF16)] * 4,
        compiler_params=params(),
        cost_estimate=HINT,
        name="in_turn",
    )(flag[None], ka, kb, va, vb)


class Order:
    def __init__(self, mark):
        self.mark = mark

    def wait(self, x):
        x, self.mark = lax.optimization_barrier((x, self.mark))
        return x

    def do(self, f, first, *args):
        return self.wait(f(self.wait(first), *args))


def pipelined_body(
    tokens, norm_gain, qkv_weight, out_weight, key_cache, value_cache, prefix_len, stretch_len
):
    gx = lax.axis_index("gx")
    z = lax.axis_index("gy")
    chip, core = gx // 2, gx % 2
    rows = tokens.shape[0]
    half = rows // 2
    width = out_weight.shape[1]
    pieces = 4
    order = Order(prefix_len)
    do, wait = order.do, order.wait

    def along(x, pairs):
        return lax.ppermute(x, "gy", pairs)

    def over_core(x):
        return lax.ppermute(x, "gx", [(i, i ^ 1) for i in range(4)])

    def over_chip(x):
        return lax.ppermute(x, "gx", [(i, i ^ 2) for i in range(4)])

    sibling = [(0, 1), (1, 0), (2, 3), (3, 2)]
    middle = [(1, 2), (2, 1)]
    outward = [(1, 0), (2, 3)]
    inward = [(0, 1), (3, 2)]
    is_mid = (z == 1) | (z == 2)

    request, second = z // 2, z % 2
    other = 1 - request
    local = jnp.arange(8, dtype=jnp.int32)
    pairs = jnp.array([0, 2, 1, 3, 9, 11, 10, 12], jnp.int32)
    tiles = jnp.concatenate(
        [
            is_mid.astype(jnp.int32)[None],
            pairs + (1 - core) * 4,
            jnp.array([8, 17], jnp.int32),
            (local // 4) * 9 + core * 4 + local % 4,
        ]
    )
    spots = jnp.stack([gx, gx ^ 1, gx ^ 2, gx ^ 3, 0 * gx]).astype(jnp.int32)
    near = jnp.stack([core, 1 - core, chip]).astype(jnp.int32)
    far = jnp.stack([core, 1 - core, 1 - chip]).astype(jnp.int32)

    def pick(flag, a, b):
        return jnp.where(flag, a, b)

    def row_squares(x):
        v = x.astype(F32)
        return jnp.sum(v * v, axis=1, keepdims=True)

    def tables(starts):
        pos = (starts[:, None] + jnp.arange(rows, dtype=jnp.int32)[None, :]).reshape(-1)
        lane = jnp.arange(HD, dtype=jnp.int32)
        freq = THETA ** (-((lane % (HD // 2)).astype(F32) * 2.0) / HD)
        angles = pos.astype(F32)[:, None] * freq[None, :]
        sign = jnp.where(lane < HD // 2, -1.0, 1.0).astype(F32)
        return jnp.cos(angles), jnp.sin(angles) * sign[None, :]

    def attention(q, req, part, ka, kb, va, vb):
        info = jnp.stack([req, chip, prefix_len[req], stretch_len[req], part]).astype(jnp.int32)
        return attend(info, q, key_cache, value_cache, ka, kb, va, vb)

    at_two = z == 2
    squares = do(row_squares, tokens)
    squares_c = over_core(squares)
    starts = jnp.stack(
        [
            prefix_len[request] + second * rows,
            prefix_len[request] + (1 - second) * rows,
            prefix_len[other],
            prefix_len[other] + rows,
        ]
    )
    squares_c = wait(squares_c)
    squares = do(lambda a: a + squares_c, squares)
    squares_x = wait(over_chip(squares))

    def normed(x, i):
        cut = slice(i * half, (i + 1) * half)
        scale = lax.rsqrt((squares + squares_x)[cut] / D + EPSILON)
        return (x[cut].astype(F32) * scale * norm_gain[None, :]).astype(BF16)

    own_a = do(lambda x: normed(x, 0), tokens)
    a0 = along(own_a, sibling)
    own_b = do(lambda x: normed(x, 1), tokens)
    a1 = along(own_b, sibling)
    *mine_o, keep_o = do(lambda x: project(tiles, [x, own_b], qkv_weight), own_a)
    recv_o = [over_core(x) for x in mine_o]
    a0 = wait(a0)
    m0 = along(do(lambda x: choose(at_two, own_a, x), a0), middle)
    cos, sin = do(tables, starts)
    a1 = wait(a1)
    m1 = along(do(lambda x: choose(at_two, own_b, x), a1), middle)
    recv_o = wait(recv_o)
    cross_o = over_chip(do(lambda x: combine(chip, keep_o, mine_o, x), recv_o))
    m0 = wait(m0)
    n0 = along(m0, outward)

    *mine_a, keep_a = do(lambda x: project(tiles, [x, a1], qkv_weight), a0)
    recv_a = [over_core(x) for x in mine_a]
    n0 = wait(n0)
    cross_o = wait(cross_o)
    m1 = wait(m1)
    n1 = along(m1, outward)
    m2 = along(do(lambda x: choose(at_two, x, own_a), a0), middle)
    recv_a = wait(recv_a)
    cross_a = over_chip(do(lambda x: combine(chip, keep_a, mine_a, x), recv_a))
    q_o, k_o, v_o = do(
        lambda x: finish(chip, keep_o, mine_o, recv_o, x, cos, sin, 0), cross_o
    )
    cross_a = wait(cross_a)
    q_a, k_a, v_a = do(
        lambda x: finish(chip, keep_a, mine_a, recv_a, x, cos, sin, 1), cross_a
    )
    own_first = (second == 0).astype(jnp.int32)
    k0, k1, v0, v1 = do(lambda k: in_turn(own_first, k_o, k, v_o, v_a), k_a)
    m2 = wait(m2)
    n2 = along(m2, outward)
    m3 = along(do(lambda x: choose(at_two, x, own_b), a1), middle)
    att_a = do(lambda q: attention(q, request, 1 - second, k0, k1, v0, v1), q_a)
    att_ax = over_chip(att_a)
    att_ac = over_core(att_a)

    n1 = wait(n1)
    *mine_b, keep_b = do(lambda x: project(tiles, [x, m1, n0, n1], qkv_weight), m0)
    recv_b = [over_core(x) for x in mine_b]
    n2 = wait(n2)
    m3 = wait(m3)
    n3 = along(m3, outward)
    att_ax = wait(att_ax)
    att_ad = over_core(att_ax)
    att_ac, att_ad = wait((att_ac, att_ad))
    recv_b = wait(recv_b)
    cross_b = over_chip(do(lambda x: combine(chip, keep_b, mine_b, x), recv_b))
    part_a = do(
        lambda a: out_project(
            spots, [a, att_ac, att_ax, att_ad], out_weight, None, 0, width, BF16, pieces
        ),
        att_a,
    )
    sum_a = [along(x, inward) for x in part_a]
    n3 = wait(n3)
    cross_b = wait(cross_b)
    q_b, k_b, v_b = do(
        lambda x: finish(chip, keep_b, mine_b, recv_b, x, cos, sin, 2), cross_b
    )
    att_b = do(lambda q: attention(q, other, 0, k_b, k_b, v_b, v_b), q_b)
    att_bx = over_chip(att_b)
    att_bc = over_core(att_b)

    *mine_c, keep_c = do(lambda x: project(tiles, [x, m3, n2, n3], qkv_weight), m2)
    recv_c = [over_core(x) for x in mine_c]
    sum_a = wait(sum_a)
    att_bx = wait(att_bx)
    att_bd = over_core(att_bx)
    att_bc, att_bd = wait((att_bc, att_bd))
    recv_c = wait(recv_c)
    cross_c = over_chip(do(lambda x: combine(chip, keep_c, mine_c, x), recv_c))
    part_b = do(
        lambda a: out_project(
            spots, [a, att_bc, att_bx, att_bd], out_weight, None, 0, width, BF16, pieces
        ),
        att_b,
    )
    b1 = [along(x, inward) for x in part_b]
    att_o = do(lambda q: attention(q, request, second, k0, k1, v0, v1), q_o)
    att_ox = over_chip(att_o)
    att_oc = over_core(att_o)
    cross_c = wait(cross_c)
    q_c, k_c, v_c = do(
        lambda x: finish(chip, keep_c, mine_c, recv_c, x, cos, sin, 3), cross_c
    )
    b2, b3, c2, c3 = [], [], [], []

    def pass_b1(i):
        b1[i] = wait(b1[i])
        b2.append(along(do(add, b1[i], part_b[i]), middle))

    def pass_b2(i):
        b2[i] = wait(b2[i])
        b3.append(along(do(add, b2[i], part_a[i]), [(1, 0)]))

    def pass_c1(i):
        c1[i] = wait(c1[i])
        c2.append(along(do(add, c1[i], part_c[i]), middle))

    def pass_c2(i):
        c2[i] = wait(c2[i])
        c3.append(along(do(add, c2[i], part_a[i]), [(2, 3)]))

    def output_own(i):
        return do(
            lambda a: out_project(
                spots,
                [a, att_oc, att_ox, att_od],
                out_weight,
                None,
                i * (width // 2),
                width // 2,
                BF16,
                pieces // 2,
            ),
            att_o,
        )

    pass_b1(0)
    att_c = do(lambda q: attention(q, other, 1, k_b, k_c, v_b, v_c), q_c)
    att_cx = over_chip(att_c)
    att_cc = over_core(att_c)
    for i in range(1, pieces):
        pass_b1(i)
    att_ox = wait(att_ox)
    att_od = over_core(att_ox)
    att_oc, att_od = wait((att_oc, att_od))
    part_o = output_own(0)
    att_cx = wait(att_cx)
    att_cd = over_core(att_cx)
    att_cc, att_cd = wait((att_cc, att_cd))
    part_c = do(
        lambda a: out_project(
            spots, [a, att_cc, att_cx, att_cd], out_weight, None, 0, width, BF16, pieces
        ),
        att_c,
    )
    c1 = [along(x, inward) for x in part_c]
    part_o += output_own(1)
    pass_b2(0)
    pass_c1(0)
    pass_b2(1)
    pass_c1(1)
    b3[0] = wait(b3[0])
    pass_c2(0)
    pass_b2(2)
    pass_c1(2)
    b3[1] = wait(b3[1])
    pass_c2(1)
    pass_b2(3)
    pass_c1(3)
    b3[2] = wait(b3[2])
    pass_c2(2)
    b3[3] = wait(b3[3])
    pass_c2(3)
    zero = jnp.zeros((), BF16)
    total = lambda *xs: sum(x.astype(F32) for x in xs).astype(BF16)
    side = lambda xs: jnp.concatenate(xs, 1)
    base = do(lambda o: total(side(o), side(sum_a), side(b3), pick(z == 2, side(b2), zero)), part_o)
    c3 = wait(c3)
    ends = (z == 1) & (order.mark[0] > 0)
    return total(base, side(c3), pick(ends, side(c2), zero))


def rotate(values, positions):
    half = values.shape[-1] // 2
    freq = THETA ** (-(jnp.arange(half, dtype=jnp.float32) * 2.0) / values.shape[-1])
    angles = positions.astype(jnp.float32)[:, None] * freq[None, :]
    cosine = jnp.concatenate([jnp.cos(angles), jnp.cos(angles)], -1)[:, None, :]
    sine = jnp.concatenate([jnp.sin(angles), jnp.sin(angles)], -1)[:, None, :]
    turned = jnp.concatenate([-values[..., half:], values[..., :half]], -1)
    return values * cosine + turned * sine


def row_positions(row_ids, prefix_len):
    request = row_ids // STRETCH
    match = request[:, None] == jnp.arange(prefix_len.shape[0], dtype=jnp.int32)[None, :]
    start = jnp.sum(jnp.where(match, prefix_len[None, :], 0), axis=1)
    return start + row_ids % STRETCH


def attend_any(
    queries, offsets, cached_keys, cached_values, fresh_keys, fresh_values, prefix, live
):
    keys = jnp.concatenate([cached_keys, fresh_keys], 0)
    values = jnp.concatenate([cached_values, fresh_values], 0)
    scores = jnp.dot(queries, keys.T, preferred_element_type=jnp.float32) * queries.shape[-1] ** (
        -0.5
    )
    span = cached_keys.shape[0]
    places = jnp.arange(keys.shape[0], dtype=jnp.int32)
    shifted = places - span
    allowed = jnp.where(
        (places < span)[None, :],
        (places < prefix)[None, :],
        (shifted[None, :] < live) & (shifted[None, :] <= offsets[:, None]),
    )
    scores = jnp.where(allowed, scores, -1e30)
    highest = jnp.max(scores, axis=1, keepdims=True)
    weights = jnp.where(allowed, jnp.exp(scores - highest), 0.0)
    total = jnp.sum(weights, axis=1, keepdims=True)
    probs = (weights / total).astype(jnp.bfloat16)
    return jnp.dot(probs, values, preferred_element_type=jnp.float32).astype(jnp.bfloat16)


def general_body(
    tokens, norm_gain, qkv_weight, out_weight, key_cache, value_cache, prefix_len, stretch_len
):
    group = QH // KVH
    index_gx = lax.axis_index("gx")
    whole = lax.all_gather(tokens, "gy", axis=0, tiled=True)
    widened = whole.astype(jnp.float32)
    squares = lax.psum(jnp.sum(widened * widened, axis=1), "gx")
    normed_all = (widened * lax.rsqrt(squares / D + EPSILON)[:, None] * norm_gain[None, :]).astype(
        jnp.bfloat16
    )
    total_rows = normed_all.shape[0]
    local_groups = qkv_weight.shape[1] // ((group + 2) * HD)
    requests = prefix_len.shape[0]
    projected = jnp.dot(normed_all, qkv_weight, preferred_element_type=jnp.float32)
    blocks = projected.reshape(total_rows, local_groups, group + 2, HD)
    query_part = blocks[:, :, :group].reshape(total_rows, local_groups * group * HD)
    pair_part = blocks[:, :, group:].reshape(total_rows, local_groups * 2 * HD)
    query_mine = lax.psum_scatter(query_part, "gx", scatter_dimension=1, tiled=True)
    pair_sums = lax.psum(pair_part, "gx")
    positions = row_positions(jnp.arange(total_rows, dtype=jnp.int32), prefix_len)
    pairs = pair_sums.reshape(total_rows, local_groups, 2, HD)
    fresh_keys = rotate(pairs[:, :, 0], positions).astype(jnp.bfloat16)
    fresh_values = pairs[:, :, 1].astype(jnp.bfloat16)
    heads_here = query_mine.shape[1] // HD
    queries = rotate(query_mine.reshape(total_rows, heads_here, HD), positions).astype(jnp.bfloat16)
    offsets = jnp.arange(STRETCH, dtype=jnp.int32)
    head_columns = []
    for head in range(heads_here):
        group_index = (index_gx * heads_here + head) // group
        request_rows = []
        for request in range(requests):
            lower = request * STRETCH
            upper = lower + STRETCH
            result = attend_any(
                queries[lower:upper, head],
                offsets,
                lax.dynamic_slice_in_dim(key_cache[request], group_index * HD, HD, 1),
                lax.dynamic_slice_in_dim(value_cache[request], group_index * HD, HD, 1),
                lax.dynamic_index_in_dim(fresh_keys[lower:upper], group_index, 1, keepdims=False),
                lax.dynamic_index_in_dim(fresh_values[lower:upper], group_index, 1, keepdims=False),
                prefix_len[request],
                stretch_len[request],
            )
            request_rows.append(result)
        head_columns.append(jnp.concatenate(request_rows, 0))
    local_out = jnp.concatenate(head_columns, 1)
    gathered_out = lax.all_gather(local_out, "gx", axis=1, tiled=True)
    summed = lax.psum_scatter(
        jnp.dot(gathered_out, out_weight, preferred_element_type=jnp.float32),
        "gy",
        scatter_dimension=0,
        tiled=True,
    )
    return summed.astype(jnp.bfloat16)


def solution(mesh):
    placed = (
        P(("groups", "gy"), "gx"),
        P("gx"),
        P("gx", "gy"),
        P("gy", "gx"),
        P("groups", None, "gy"),
        P("groups", None, "gy"),
        P("groups"),
        P("groups"),
    )
    fits = mesh.shape["gx"] == 4 and mesh.shape["gy"] == 4
    return jax.shard_map(
        pipelined_body if fits else general_body,
        mesh=mesh,
        in_specs=placed,
        out_specs=P(("groups", "gy"), "gx"),
        check_vma=False,
    )
```

```python
import math

import jax
import jax.numpy as jnp
from jax import lax
from jax.experimental import pallas as pl
from jax.experimental.pallas import tpu as pltpu
from jax.sharding import PartitionSpec as P

D = 16384
QH = 128
KVH = 8
HD = 128
STRETCH = 512
G = QH // KVH

THETA = 500000.0
EPSILON = 1e-05
QSCALE = HD ** (-0.5) * math.log2(math.e)

F32 = jnp.float32
BF16 = jnp.bfloat16
TILE = 256
VMEM_LIMIT = 56 * 1024 * 1024


HINT = pl.CostEstimate(flops=1024, bytes_accessed=1024, transcendentals=0)


def params(**kw):
    return pltpu.CompilerParams(vmem_limit_bytes=VMEM_LIMIT, **kw)


def sds(shape, dtype):
    return jax.ShapeDtypeStruct(shape, dtype)


def whole(*_):
    return (0, 0)


PER = 2


def project_kernel(s_ref, *refs, pieces, sources, blocks):
    x_refs, refs = refs[:sources], refs[sources:]
    w_refs, refs = refs[:PER], refs[PER:]
    out_refs, (x_ref, sem) = refs[:-2], refs[-2:]
    step = pl.program_id(0)
    half = x_refs[0].shape[0]
    rows = x_ref.shape[0] // blocks

    def fetch(group):
        copies = [
            pltpu.make_async_copy(ref, x_ref.at[pl.ds(i * half, half)], sem.at[i])
            for i, ref in enumerate(group)
        ]
        for c in copies:
            c.start()
        for c in copies:
            c.wait()

    @pl.when(step == 0)
    def _():
        if sources == pieces:
            fetch(x_refs)
        else:

            @pl.when(s_ref[0] == 1)
            def _():
                fetch(x_refs[:pieces])

            @pl.when(s_ref[0] == 0)
            def _():
                fetch(x_refs[pieces:])

    peer_steps = 10 // PER
    products = [jnp.dot(x_ref[...], w[...], preferred_element_type=F32) for w in w_refs]

    @pl.when(step < peer_steps)
    def _():
        for b in range(blocks):
            for i, v in enumerate(products):
                out_refs[3 * b + i][...] = v[b * rows : (b + 1) * rows].astype(BF16)

    @pl.when(step >= peer_steps)
    def _():
        for b in range(blocks):
            for i, v in enumerate(products):
                cut = slice(i * TILE, (i + 1) * TILE)
                out_refs[3 * b + 2][:, cut] = v[b * rows : (b + 1) * rows]


def project(info, xs, w, pieces=2):
    half, depth = xs[0].shape
    peer_steps = 10 // PER
    steps = 18 // PER
    blocks = pieces // 2
    weights = [
        pl.BlockSpec((depth, TILE), lambda j, s, i=i: (0, s[1 + j * PER + i])) for i in range(PER)
    ]
    rows = 2 * half
    peer = pl.BlockSpec((rows, TILE), lambda j, s: (0, jnp.minimum(j, peer_steps - 1)))
    own = pl.BlockSpec((rows, PER * TILE), lambda j, s: (0, jnp.maximum(j - peer_steps, 0)))
    out = pl.pallas_call(
        lambda *refs: project_kernel(*refs, pieces=pieces, sources=len(xs), blocks=blocks),
        grid_spec=pltpu.PrefetchScalarGridSpec(
            num_scalar_prefetch=1,
            grid=(steps,),
            in_specs=[pl.BlockSpec(memory_space=pl.ANY)] * len(xs) + weights,
            out_specs=[peer, peer, own] * blocks,
            scratch_shapes=[
                pltpu.VMEM((half * pieces, depth), BF16),
                pltpu.SemaphoreType.DMA((pieces,)),
            ],
        ),
        out_shape=[
            sds((rows, 5 * TILE), BF16),
            sds((rows, 5 * TILE), BF16),
            sds((rows, 8 * TILE), F32),
        ]
        * blocks,
        compiler_params=params(),
        cost_estimate=HINT,
        name="project",
    )(info, *xs, *([w] * PER))
    return out


def core_sums(s_ref, own_ref, kv_refs, recv_refs):
    n = recv_refs[0].shape[1]
    first = s_ref[0] == 0
    mine = jnp.where(first, kv_refs[0][...].astype(F32), kv_refs[1][...].astype(F32))
    theirs = jnp.where(first, kv_refs[2][...].astype(F32), kv_refs[3][...].astype(F32))
    halves = [
        own_ref[:, i * n : (i + 1) * n] + r[...].astype(F32) for i, r in enumerate(recv_refs)
    ]
    return halves, mine + theirs


def combine_kernel(s_ref, own_ref, kva_ref, kvb_ref, ra_ref, rb_ref, rka_ref, rkb_ref, o_ref):
    halves, kv = core_sums(s_ref, own_ref, (kva_ref, kvb_ref, rka_ref, rkb_ref), (ra_ref, rb_ref))
    n = ra_ref.shape[1]
    for i, v in enumerate(halves):
        o_ref[:, i * n : (i + 1) * n] = v.astype(BF16)
    o_ref[:, 2 * n :] = kv.astype(BF16)


def sums_specs(rows, n):
    kv = pl.BlockSpec((rows, TILE), lambda i, s: (i, 4))
    half = pl.BlockSpec((rows, n // 2), lambda i, s: (i, s[0]))
    return [pl.BlockSpec((rows, n), lambda i, s: (i, s[0])), kv, kv, half, half, kv, kv]


def combine(chip, own, mine, recv):
    rows = own.shape[0]
    n = own.shape[1] // 2
    part = rows // 2
    other = jnp.reshape(1 - chip, (1,)).astype(jnp.int32)
    return pl.pallas_call(
        combine_kernel,
        grid_spec=pltpu.PrefetchScalarGridSpec(
            num_scalar_prefetch=1,
            grid=(rows // part,),
            in_specs=sums_specs(part, n),
            out_specs=pl.BlockSpec((part, n + TILE), lambda i, s: (i, 0)),
        ),
        out_shape=sds((rows, n + TILE), BF16),
        compiler_params=params(),
        cost_estimate=HINT,
        name="combine",
    )(other, own, *mine, *recv, *recv)


def finish_kernel(s_ref, own_ref, kva_ref, kvb_ref, ra_ref, rb_ref, rka_ref, rkb_ref, *rest):
    x_ref, cos_ref, sin_ref, q_ref, k_ref, v_ref = rest
    halves, kv = core_sums(s_ref, own_ref, (kva_ref, kvb_ref, rka_ref, rkb_ref), (ra_ref, rb_ref))
    n = ra_ref.shape[1]
    cos, sin = cos_ref[...], sin_ref[...]

    def turn(v):
        return v * cos + pltpu.roll(v, HD // 2, 1) * sin

    for i, half in enumerate(halves):
        v = half + x_ref[:, i * n : (i + 1) * n].astype(F32)
        for h in range(n // HD):
            at = i * (n // HD) + h
            q_ref[at] = (turn(v[:, h * HD : (h + 1) * HD]) * QSCALE).astype(BF16)
    kv += x_ref[:, 2 * n :].astype(F32)
    k_ref[...] = turn(kv[:, :HD]).astype(BF16)
    v_ref[...] = kv[:, HD:].astype(BF16)


def finish(chip, own, mine, recv, cross, cos, sin, slot):
    rows = own.shape[0]
    n = own.shape[1] // 2
    part = rows // 2
    here = jnp.reshape(chip, (1,)).astype(jnp.int32)
    row = lambda i, s: (i, 0)
    table = lambda i, s: (slot * (rows // part) + i, 0)
    return pl.pallas_call(
        finish_kernel,
        grid_spec=pltpu.PrefetchScalarGridSpec(
            num_scalar_prefetch=1,
            grid=(rows // part,),
            in_specs=sums_specs(part, n)
            + [
                pl.BlockSpec((part, n + TILE), row),
                pl.BlockSpec((part, HD), table),
                pl.BlockSpec((part, HD), table),
            ],
            out_specs=[
                pl.BlockSpec((n // HD, part, HD), lambda i, s: (0, i, 0)),
                pl.BlockSpec((part, HD), row),
                pl.BlockSpec((part, HD), row),
            ],
        ),
        out_shape=[sds((n // HD, rows, HD), BF16), sds((rows, HD), BF16), sds((rows, HD), BF16)],
        compiler_params=params(),
        cost_estimate=HINT,
        name="finish",
    )(here, own, *mine, *recv, *recv, cross, cos, sin)


KB = 512
CHUNK = 1024
PIECE = 512
LARGE = 2.0**100


def attend_kernel(
    s_ref, q_ref, k_ref, v_ref, ka_ref, kb_ref, va_ref, vb_ref, o_ref, vx_ref, acc_ref, top_ref, at
):
    prefix, live, half = s_ref[at + 2], s_ref[at + 3], s_ref[at + 4]
    rows = ka_ref.shape[0]
    m_rows = q_ref.shape[0]
    span = k_ref.shape[1]
    fresh = 2 * rows
    vx_ref[:span, :HD] = v_ref[0]
    vx_ref[span : span + rows, :HD] = va_ref[...]
    vx_ref[span + rows :, :HD] = vb_ref[...]
    vx_ref[:, HD:] = jnp.ones((span + fresh, HD), BF16)
    nt = (((1,), (1,)), ((), ()))
    count = prefix // KB
    rest = prefix - count * KB

    def product(a, b):
        return lax.dot_general(a, b, nt, preferred_element_type=F32)

    def scores(cut, at):
        return product(q_ref[cut, :], k_ref[0, pl.ds(at, KB), :])

    def fresh_scores(cut):
        row = lax.broadcasted_iota(jnp.int32, (rows, fresh), 0) + half * rows
        place = lax.broadcasted_iota(jnp.int32, (rows, fresh), 1)
        ok = (place <= row) & (place < live)
        q = q_ref[cut, :]
        s = jnp.concatenate([product(q, ka_ref[...]), product(q, kb_ref[...])], 1)
        s = s.reshape(PIECE // rows, rows, fresh)
        return jnp.where(ok[None], s, -1e30).reshape(PIECE, fresh)

    def rest_scores(cut, at):
        place = lax.broadcasted_iota(jnp.int32, (PIECE, KB), 1)
        return jnp.where(place < rest, scores(cut, at), -1e30)

    def add(s, cut, at):
        p = jnp.exp2(s - top_ref[cut, :1]).astype(BF16)
        acc_ref[cut, :] += jnp.dot(p, vx_ref[pl.ds(at, KB), :], preferred_element_type=F32)

    def raise_top(s, cut):
        top_ref[cut, :] = jnp.maximum(top_ref[cut, :], jnp.max(s, axis=1, keepdims=True))

    def block(i):
        return pl.multiple_of(i * KB, KB)

    def cuts(size, visit):
        def step(i, carry):
            visit(pl.ds(pl.multiple_of(i * size, size), size))
            return carry

        lax.fori_loop(0, m_rows // size, step, 0)

    def blocks(stop, visit):
        def step(i, carry):
            visit(block(i))
            return carry

        lax.fori_loop(0, stop, step, 0)

    def sweep():
        acc_ref[...] = jnp.zeros_like(acc_ref)
        cuts(PIECE, lambda cut: add(fresh_scores(cut), cut, span))

        @pl.when(rest > 0)
        def _():
            last = block(count)
            cuts(PIECE, lambda cut: add(rest_scores(cut, last), cut, last))

        cuts(CHUNK, lambda cut: blocks(count, lambda at: add(scores(cut, at), cut, at)))

    top_ref[...] = jnp.full(top_ref.shape, -1e30, F32)
    cuts(PIECE, lambda cut: raise_top(scores(cut, 0), cut))

    def attempt(i):
        @pl.when(i > 0)
        def _():
            cuts(PIECE, lambda cut: raise_top(fresh_scores(cut), cut))
            cuts(PIECE, lambda cut: blocks(count, lambda at: raise_top(scores(cut, at), cut)))

            @pl.when(rest > 0)
            def _():
                last = block(count)
                cuts(PIECE, lambda cut: raise_top(rest_scores(cut, last), cut))

        sweep()
        return jnp.max(jnp.where(acc_ref[:, HD:] < LARGE, 0.0, 1.0))

    def more(state):
        return (state[0] == 0) | ((state[0] == 1) & (state[1] > 0.0))

    lax.while_loop(more, lambda state: (state[0] + 1, attempt(state[0])), (0, 0.0))

    for h in range(m_rows // rows):
        cut = slice(h * rows, (h + 1) * rows)
        o_ref[:, h * HD : (h + 1) * HD] = (acc_ref[cut, :HD] / acc_ref[cut, HD:]).astype(BF16)


def attend(info, slot, q, key_cache, value_cache, ka, kb, va, vb):
    heads, rows, _ = q.shape
    span = key_cache.shape[1]
    m_rows = heads * rows
    at = 5 * slot
    q = q.reshape(m_rows, HD)
    cache = pl.BlockSpec((1, span, HD), lambda i, s: (s[at], 0, s[at + 1]))
    fresh = pl.BlockSpec((rows, HD), whole)
    return pl.pallas_call(
        lambda *refs: attend_kernel(*refs, at=at),
        grid_spec=pltpu.PrefetchScalarGridSpec(
            num_scalar_prefetch=1,
            grid=(1,),
            in_specs=[
                pl.BlockSpec((m_rows, HD), whole),
                cache,
                cache,
                fresh,
                fresh,
                fresh,
                fresh,
            ],
            out_specs=pl.BlockSpec((rows, heads * HD), whole),
            scratch_shapes=[
                pltpu.VMEM((span + 2 * rows, 2 * HD), BF16),
                pltpu.VMEM((m_rows, 2 * HD), F32),
                pltpu.VMEM((m_rows, HD), F32),
            ],
        ),
        out_shape=sds((rows, heads * HD), BF16),
        compiler_params=params(),
        cost_estimate=HINT,
        name="attend",
    )(info, q, key_cache, value_cache, ka, kb, va, vb)


def out_kernel(s_ref, *refs, sources, before, outs):
    a_refs, refs = refs[:sources], refs[sources:]
    x_ref, sem = refs[-2:]
    o_refs = refs[-2 - outs : -2]
    depth = a_refs[0].shape[1]

    @pl.when(pl.program_id(0) == 0)
    def _():
        copies = [
            pltpu.make_async_copy(
                ref, x_ref.at[:, pl.ds(pl.multiple_of(s_ref[i] * depth, depth), depth)], sem.at[i]
            )
            for i, ref in enumerate(a_refs)
        ]
        for c in copies:
            c.start()
        for c in copies:
            c.wait()

    total = jnp.dot(x_ref[...], refs[0][...], preferred_element_type=F32)
    if before:
        total += refs[1][...]
    for i, o_ref in enumerate(o_refs):

        @pl.when(pl.program_id(0) * outs // pl.num_programs(0) == i)
        def _():
            o_ref[...] = total.astype(o_ref.dtype)


def out_project(index, pieces, w, before, first, width, dtype, outs=1, cols=1024):
    rows, depth = pieces[0].shape
    n = len(pieces)
    start = first // cols
    cols = min(cols, width)
    specs = [pl.BlockSpec(memory_space=pl.ANY)] * n + [
        pl.BlockSpec((n * depth, cols), lambda j, s: (s[n], start + j))
    ]
    operands = list(pieces) + [w]
    if before is not None:
        operands.append(before)
        specs.append(pl.BlockSpec((rows, cols), lambda j, s: (0, start + j)))
    each = width // cols // outs
    out = pl.pallas_call(
        lambda *refs: out_kernel(*refs, sources=n, before=before is not None, outs=outs),
        grid_spec=pltpu.PrefetchScalarGridSpec(
            num_scalar_prefetch=1,
            grid=(width // cols,),
            in_specs=specs,
            out_specs=[
                pl.BlockSpec((rows, cols), lambda j, s, i=i: (0, jnp.clip(j - i * each, 0, each - 1)))
                for i in range(outs)
            ],
            scratch_shapes=[pltpu.VMEM((rows, n * depth), BF16), pltpu.SemaphoreType.DMA((n,))],
        ),
        out_shape=[sds((rows, width // outs), dtype)] * outs,
        compiler_params=params(),
        cost_estimate=HINT,
        name="out_project",
    )(index, *operands)
    return out[0] if outs == 1 else out


def choose_kernel(s_ref, a_ref, b_ref, o_ref):
    o_ref[...] = jnp.where(s_ref[0] == 1, a_ref[...], b_ref[...])


def choose(flag, a, b):
    rows, cols = a.shape
    part = rows // 2
    block = pl.BlockSpec((part, cols), lambda i, s: (i, 0))
    return pl.pallas_call(
        choose_kernel,
        grid_spec=pltpu.PrefetchScalarGridSpec(
            num_scalar_prefetch=1,
            grid=(rows // part,),
            in_specs=[block] * 2,
            out_specs=block,
        ),
        out_shape=sds(a.shape, a.dtype),
        compiler_params=params(),
        cost_estimate=HINT,
        name="choose",
    )(flag.astype(jnp.int32)[None], a, b)


def add_kernel(a_ref, b_ref, o_ref):
    o_ref[...] = (a_ref[...].astype(F32) + b_ref[...].astype(F32)).astype(BF16)


def add(a, b, part=0, cuts=1):
    shape = (a.shape[0], a.shape[1] // cuts)
    there = pl.BlockSpec(shape, lambda i: (0, part))
    block = pl.BlockSpec(shape, lambda i: (0, 0))
    return pl.pallas_call(
        add_kernel,
        grid=(1,),
        in_specs=[block if cuts == 1 else there, there],
        out_specs=block,
        out_shape=sds(shape, BF16),
        compiler_params=params(),
        cost_estimate=HINT,
        name="add",
    )(a, b)


def in_turn_kernel(s_ref, ka_ref, kb_ref, va_ref, vb_ref, k0_ref, k1_ref, v0_ref, v1_ref):
    first = s_ref[0] == 1

    @pl.when(first)
    def _():
        k0_ref[...], k1_ref[...] = ka_ref[...], kb_ref[...]
        v0_ref[...], v1_ref[...] = va_ref[...], vb_ref[...]

    @pl.when(jnp.logical_not(first))
    def _():
        k0_ref[...], k1_ref[...] = kb_ref[...], ka_ref[...]
        v0_ref[...], v1_ref[...] = vb_ref[...], va_ref[...]


def in_turn(flag, ka, kb, va, vb):
    block = pl.BlockSpec(ka.shape, whole)
    return pl.pallas_call(
        in_turn_kernel,
        grid_spec=pltpu.PrefetchScalarGridSpec(
            num_scalar_prefetch=1, grid=(1,), in_specs=[block] * 4, out_specs=[block] * 4
        ),
        out_shape=[sds(ka.shape, BF16)] * 4,
        compiler_params=params(),
        cost_estimate=HINT,
        name="in_turn",
    )(flag[None], ka, kb, va, vb)


class Order:
    def __init__(self, mark):
        self.mark = mark

    def wait(self, x):
        x, self.mark = lax.optimization_barrier((x, self.mark))
        return x

    def do(self, f, first, *args):
        return self.wait(f(self.wait(first), *args))


def pipelined_body(
    tokens, norm_gain, qkv_weight, out_weight, key_cache, value_cache, prefix_len, stretch_len
):
    gx = lax.axis_index("gx")
    z = lax.axis_index("gy")
    chip, core = gx // 2, gx % 2
    rows = tokens.shape[0]
    half = rows // 2
    width = out_weight.shape[1]
    pieces = 4
    order = Order(prefix_len)
    do, wait = order.do, order.wait

    def along(x, pairs):
        return lax.ppermute(x, "gy", pairs)

    def over_core(x):
        return lax.ppermute(x, "gx", [(i, i ^ 1) for i in range(4)])

    def over_chip(x):
        return lax.ppermute(x, "gx", [(i, i ^ 2) for i in range(4)])

    sibling = [(0, 1), (1, 0), (2, 3), (3, 2)]
    middle = [(1, 2), (2, 1)]
    outward = [(1, 0), (2, 3)]
    inward = [(0, 1), (3, 2)]
    is_mid = (z == 1) | (z == 2)

    request, second = z // 2, z % 2
    other = 1 - request
    local = jnp.arange(8, dtype=jnp.int32)
    pairs = jnp.array([0, 2, 1, 3, 9, 11, 10, 12], jnp.int32)
    tiles = jnp.concatenate(
        [
            is_mid.astype(jnp.int32)[None],
            pairs + (1 - core) * 4,
            jnp.array([8, 17], jnp.int32),
            (local // 4) * 9 + core * 4 + local % 4,
        ]
    )
    spots = jnp.stack([gx, gx ^ 1, gx ^ 2, gx ^ 3, 0 * gx]).astype(jnp.int32)
    near = jnp.stack([core, 1 - core, chip]).astype(jnp.int32)
    far = jnp.stack([core, 1 - core, 1 - chip]).astype(jnp.int32)

    def pick(flag, a, b):
        return jnp.where(flag, a, b)

    def row_squares(x):
        v = x.astype(F32)
        return jnp.sum(v * v, axis=1, keepdims=True)

    def tables(starts):
        pos = (starts[:, None] + jnp.arange(rows, dtype=jnp.int32)[None, :]).reshape(-1)
        lane = jnp.arange(HD, dtype=jnp.int32)
        freq = THETA ** (-((lane % (HD // 2)).astype(F32) * 2.0) / HD)
        angles = pos.astype(F32)[:, None] * freq[None, :]
        sign = jnp.where(lane < HD // 2, -1.0, 1.0).astype(F32)
        return jnp.cos(angles), jnp.sin(angles) * sign[None, :]

    parts = [(request, second), (request, 1 - second), (other, 0 * z), (other, 0 * z + 1)]

    def numbers(prefix):
        values = [
            v for req, part in parts for v in (req, chip, prefix[req], stretch_len[req], part)
        ]
        return jnp.stack(values).astype(jnp.int32)

    def attention(slot, q, ka, kb, va, vb):
        return attend(info, slot, q, key_cache, value_cache, ka, kb, va, vb)

    at_two = z == 2
    squares = do(row_squares, tokens)
    squares_c = over_core(squares)
    starts = jnp.stack(
        [
            prefix_len[request] + second * rows,
            prefix_len[request] + (1 - second) * rows,
            prefix_len[other],
            prefix_len[other] + rows,
        ]
    )
    squares_c = wait(squares_c)
    squares = do(lambda a: a + squares_c, squares)
    squares_x = wait(over_chip(squares))

    def normed(x, i):
        cut = slice(i * half, (i + 1) * half)
        scale = lax.rsqrt((squares + squares_x)[cut] / D + EPSILON)
        return (x[cut].astype(F32) * scale * norm_gain[None, :]).astype(BF16)

    own_a = do(lambda x: normed(x, 0), tokens)
    a0 = along(own_a, sibling)
    own_b = do(lambda x: normed(x, 1), tokens)
    a1 = along(own_b, sibling)
    *mine_o, keep_o = do(lambda x: project(tiles, [x, own_b], qkv_weight), own_a)
    recv_o = [over_core(x) for x in mine_o]
    a0 = wait(a0)
    m0 = along(do(lambda x: choose(at_two, own_a, x), a0), middle)
    cos, sin = do(tables, starts)
    info = do(numbers, prefix_len)
    recv_o = wait(recv_o)
    cross_o = over_chip(do(lambda x: combine(chip, keep_o, mine_o, x), recv_o))
    a1 = wait(a1)
    m1 = along(do(lambda x: choose(at_two, own_b, x), a1), middle)
    m0 = wait(m0)
    n0 = along(m0, outward)

    *mine_a, keep_a = do(lambda x: project(tiles, [x, a1], qkv_weight), a0)
    recv_a = [over_core(x) for x in mine_a]
    n0 = wait(n0)
    cross_o = wait(cross_o)
    m1 = wait(m1)
    n1 = along(m1, outward)
    m2 = along(do(lambda x: choose(at_two, x, own_a), a0), middle)
    recv_a = wait(recv_a)
    cross_a = over_chip(do(lambda x: combine(chip, keep_a, mine_a, x), recv_a))
    q_o, k_o, v_o = do(
        lambda x: finish(chip, keep_o, mine_o, recv_o, x, cos, sin, 0), cross_o
    )
    n1 = wait(n1)
    cross_a = wait(cross_a)
    q_a, k_a, v_a = do(
        lambda x: finish(chip, keep_a, mine_a, recv_a, x, cos, sin, 1), cross_a
    )
    own_first = (second == 0).astype(jnp.int32)
    k0, k1, v0, v1 = do(lambda k: in_turn(own_first, k_o, k, v_o, v_a), k_a)
    m2 = wait(m2)
    n2 = along(m2, outward)
    m3 = along(do(lambda x: choose(at_two, x, own_b), a1), middle)
    att_a = do(lambda q: attention(1, q, k0, k1, v0, v1), q_a)
    att_ax = over_chip(att_a)
    att_ac = over_core(att_a)
    m3 = wait(m3)
    n3 = along(m3, outward)
    att_o = do(lambda q: attention(0, q, k0, k1, v0, v1), q_o)
    att_ox = over_chip(att_o)
    att_oc = over_core(att_o)
    n2 = wait(n2)
    att_ax = wait(att_ax)
    att_ad = over_core(att_ax)
    att_ac, att_ad = wait((att_ac, att_ad))
    part_a = do(
        lambda a: out_project(
            spots, [a, att_ac, att_ax, att_ad], out_weight, None, 0, width, BF16, 2
        ),
        att_a,
    )
    sum_a = [along(x, inward) for x in part_a]

    att_ox = wait(att_ox)
    att_od = over_core(att_ox)
    n3 = wait(n3)
    out = do(
        lambda x: project(tiles, [x, m1, m2, m3, n0, n1, n2, n3], qkv_weight, 4), m0
    )
    *mine_b, keep_b = out[:3]
    *mine_c, keep_c = out[3:]
    recv_b = [over_core(x) for x in mine_b]
    recv_c = [over_core(x) for x in mine_c]
    att_oc, att_od = wait((att_oc, att_od))
    sum_a[0] = wait(sum_a[0])
    recv_b = wait(recv_b)
    cross_b = over_chip(do(lambda x: combine(chip, keep_b, mine_b, x), recv_b))
    recv_c = wait(recv_c)
    cross_c = over_chip(do(lambda x: combine(chip, keep_c, mine_c, x), recv_c))
    def output_own(i):
        cut = width // 2
        return do(
            lambda a: out_project(
                spots, [a, att_oc, att_ox, att_od], out_weight, None, i * cut, cut, BF16, 2
            ),
            att_o,
        )

    part_o = output_own(0)
    sum_a[1] = wait(sum_a[1])
    cross_b = wait(cross_b)
    q_b, k_b, v_b = do(
        lambda x: finish(chip, keep_b, mine_b, recv_b, x, cos, sin, 2), cross_b
    )
    att_b = do(lambda q: attention(2, q, k_b, k_b, v_b, v_b), q_b)
    att_bx = over_chip(att_b)
    att_bc = over_core(att_b)
    cross_c = wait(cross_c)
    q_c, k_c, v_c = do(
        lambda x: finish(chip, keep_c, mine_c, recv_c, x, cos, sin, 3), cross_c
    )
    att_c = do(lambda q: attention(3, q, k_b, k_c, v_b, v_c), q_c)
    att_cx = over_chip(att_c)
    att_cc = over_core(att_c)
    att_bx = wait(att_bx)
    att_bd = over_core(att_bx)
    att_bc, att_bd = wait((att_bc, att_bd))
    part_b = do(
        lambda a: out_project(
            spots, [a, att_bc, att_bx, att_bd], out_weight, None, 0, width, BF16, pieces
        ),
        att_b,
    )
    b1 = [along(x, inward) for x in part_b]
    att_cx = wait(att_cx)
    att_cd = over_core(att_cx)
    att_cc, att_cd = wait((att_cc, att_cd))
    part_c = do(
        lambda a: out_project(
            spots, [a, att_cc, att_cx, att_cd], out_weight, None, 0, width, BF16, 2
        ),
        att_c,
    )
    c1 = [along(x, inward) for x in part_c]
    b2, b3, c2, c3 = [], [], [], []

    def pass_b1(i):
        b1[i] = wait(b1[i])
        b2.append(along(do(add, b1[i], part_b[i]), middle))

    def pass_b2(i):
        b2[i] = wait(b2[i])
        b3.append(along(do(add, b2[i], part_a[i // 2], i % 2), [(1, 0)]))

    def pass_c1(i):
        c1[i // 2] = wait(c1[i // 2])
        c2.append(along(do(add, c1[i // 2], part_c[i // 2], i % 2, 2), middle))

    def pass_c2(i):
        c2[i] = wait(c2[i])
        c3.append(along(do(add, c2[i], part_a[i // 2], i % 2), [(2, 3)]))

    pass_b1(0)
    pass_b1(1)
    pass_b1(2)
    part_o += output_own(1)
    pass_b1(3)
    pass_b2(0)
    pass_b2(1)
    pass_c1(0)
    pass_c1(1)
    pass_b2(2)
    pass_b2(3)
    pass_c2(0)
    pass_c2(1)
    b3[0] = wait(b3[0])
    b3[1] = wait(b3[1])
    pass_c1(2)
    pass_c1(3)
    b3[2] = wait(b3[2])
    pass_c2(2)
    b3[3] = wait(b3[3])
    pass_c2(3)
    zero = jnp.zeros((), BF16)
    total = lambda *xs: sum(x.astype(F32) for x in xs).astype(BF16)
    side = lambda xs: jnp.concatenate(xs, 1)
    base = do(lambda o: total(side(o), side(sum_a), side(b3), pick(z == 2, side(b2), zero)), part_o)
    c3 = wait(c3)
    ends = (z == 1) & (order.mark[0] > 0)
    return total(base, side(c3), pick(ends, side(c2), zero))


def rotate(values, positions):
    half = values.shape[-1] // 2
    freq = THETA ** (-(jnp.arange(half, dtype=jnp.float32) * 2.0) / values.shape[-1])
    angles = positions.astype(jnp.float32)[:, None] * freq[None, :]
    cosine = jnp.concatenate([jnp.cos(angles), jnp.cos(angles)], -1)[:, None, :]
    sine = jnp.concatenate([jnp.sin(angles), jnp.sin(angles)], -1)[:, None, :]
    turned = jnp.concatenate([-values[..., half:], values[..., :half]], -1)
    return values * cosine + turned * sine


def row_positions(row_ids, prefix_len):
    request = row_ids // STRETCH
    match = request[:, None] == jnp.arange(prefix_len.shape[0], dtype=jnp.int32)[None, :]
    start = jnp.sum(jnp.where(match, prefix_len[None, :], 0), axis=1)
    return start + row_ids % STRETCH


def attend_any(
    queries, offsets, cached_keys, cached_values, fresh_keys, fresh_values, prefix, live
):
    keys = jnp.concatenate([cached_keys, fresh_keys], 0)
    values = jnp.concatenate([cached_values, fresh_values], 0)
    scores = jnp.dot(queries, keys.T, preferred_element_type=jnp.float32) * queries.shape[-1] ** (
        -0.5
    )
    span = cached_keys.shape[0]
    places = jnp.arange(keys.shape[0], dtype=jnp.int32)
    shifted = places - span
    allowed = jnp.where(
        (places < span)[None, :],
        (places < prefix)[None, :],
        (shifted[None, :] < live) & (shifted[None, :] <= offsets[:, None]),
    )
    scores = jnp.where(allowed, scores, -1e30)
    highest = jnp.max(scores, axis=1, keepdims=True)
    weights = jnp.where(allowed, jnp.exp(scores - highest), 0.0)
    total = jnp.sum(weights, axis=1, keepdims=True)
    probs = (weights / total).astype(jnp.bfloat16)
    return jnp.dot(probs, values, preferred_element_type=jnp.float32).astype(jnp.bfloat16)


def general_body(
    tokens, norm_gain, qkv_weight, out_weight, key_cache, value_cache, prefix_len, stretch_len
):
    group = QH // KVH
    index_gx = lax.axis_index("gx")
    whole = lax.all_gather(tokens, "gy", axis=0, tiled=True)
    widened = whole.astype(jnp.float32)
    squares = lax.psum(jnp.sum(widened * widened, axis=1), "gx")
    normed_all = (widened * lax.rsqrt(squares / D + EPSILON)[:, None] * norm_gain[None, :]).astype(
        jnp.bfloat16
    )
    total_rows = normed_all.shape[0]
    local_groups = qkv_weight.shape[1] // ((group + 2) * HD)
    requests = prefix_len.shape[0]
    projected = jnp.dot(normed_all, qkv_weight, preferred_element_type=jnp.float32)
    blocks = projected.reshape(total_rows, local_groups, group + 2, HD)
    query_part = blocks[:, :, :group].reshape(total_rows, local_groups * group * HD)
    pair_part = blocks[:, :, group:].reshape(total_rows, local_groups * 2 * HD)
    query_mine = lax.psum_scatter(query_part, "gx", scatter_dimension=1, tiled=True)
    pair_sums = lax.psum(pair_part, "gx")
    positions = row_positions(jnp.arange(total_rows, dtype=jnp.int32), prefix_len)
    pairs = pair_sums.reshape(total_rows, local_groups, 2, HD)
    fresh_keys = rotate(pairs[:, :, 0], positions).astype(jnp.bfloat16)
    fresh_values = pairs[:, :, 1].astype(jnp.bfloat16)
    heads_here = query_mine.shape[1] // HD
    queries = rotate(query_mine.reshape(total_rows, heads_here, HD), positions).astype(jnp.bfloat16)
    offsets = jnp.arange(STRETCH, dtype=jnp.int32)
    head_columns = []
    for head in range(heads_here):
        group_index = (index_gx * heads_here + head) // group
        request_rows = []
        for request in range(requests):
            lower = request * STRETCH
            upper = lower + STRETCH
            result = attend_any(
                queries[lower:upper, head],
                offsets,
                lax.dynamic_slice_in_dim(key_cache[request], group_index * HD, HD, 1),
                lax.dynamic_slice_in_dim(value_cache[request], group_index * HD, HD, 1),
                lax.dynamic_index_in_dim(fresh_keys[lower:upper], group_index, 1, keepdims=False),
                lax.dynamic_index_in_dim(fresh_values[lower:upper], group_index, 1, keepdims=False),
                prefix_len[request],
                stretch_len[request],
            )
            request_rows.append(result)
        head_columns.append(jnp.concatenate(request_rows, 0))
    local_out = jnp.concatenate(head_columns, 1)
    gathered_out = lax.all_gather(local_out, "gx", axis=1, tiled=True)
    summed = lax.psum_scatter(
        jnp.dot(gathered_out, out_weight, preferred_element_type=jnp.float32),
        "gy",
        scatter_dimension=0,
        tiled=True,
    )
    return summed.astype(jnp.bfloat16)


def solution(mesh):
    placed = (
        P(("groups", "gy"), "gx"),
        P("gx"),
        P("gx", "gy"),
        P("gy", "gx"),
        P("groups", None, "gy"),
        P("groups", None, "gy"),
        P("groups"),
        P("groups"),
    )
    fits = mesh.shape["gx"] == 4 and mesh.shape["gy"] == 4
    return jax.shard_map(
        pipelined_body if fits else general_body,
        mesh=mesh,
        in_specs=placed,
        out_specs=P(("groups", "gy"), "gx"),
        check_vma=False,
    )
```

```python
import math

import jax
import jax.numpy as jnp
from jax import lax
from jax.experimental import pallas as pl
from jax.experimental.pallas import tpu as pltpu
from jax.sharding import PartitionSpec as P

D = 16384
QH = 128
KVH = 8
HD = 128
STRETCH = 512
G = QH // KVH

THETA = 500000.0
EPSILON = 1e-05
QSCALE = HD ** (-0.5) * math.log2(math.e)

F32 = jnp.float32
BF16 = jnp.bfloat16
TILE = 256
VMEM_LIMIT = 56 * 1024 * 1024


HINT = pl.CostEstimate(flops=1024, bytes_accessed=1024, transcendentals=0)


def params(**kw):
    return pltpu.CompilerParams(vmem_limit_bytes=VMEM_LIMIT, **kw)


def sds(shape, dtype):
    return jax.ShapeDtypeStruct(shape, dtype)


def whole(*_):
    return (0, 0)


PER = 2


def project_kernel(s_ref, *refs, pieces, sources, blocks):
    x_refs, refs = refs[:sources], refs[sources:]
    w_refs, refs = refs[:PER], refs[PER:]
    out_refs, (x_ref, sem) = refs[:-2], refs[-2:]
    step = pl.program_id(0)
    half = x_refs[0].shape[0]
    rows = x_ref.shape[0] // blocks

    def fetch(group):
        copies = [
            pltpu.make_async_copy(ref, x_ref.at[pl.ds(i * half, half)], sem.at[i])
            for i, ref in enumerate(group)
        ]
        for c in copies:
            c.start()
        for c in copies:
            c.wait()

    @pl.when(step == 0)
    def _():
        if sources == pieces:
            fetch(x_refs)
        else:

            @pl.when(s_ref[0] == 1)
            def _():
                fetch(x_refs[:pieces])

            @pl.when(s_ref[0] == 0)
            def _():
                fetch(x_refs[pieces:])

    peer_steps = 10 // PER
    products = [jnp.dot(x_ref[...], w[...], preferred_element_type=F32) for w in w_refs]

    @pl.when(step < peer_steps)
    def _():
        for b in range(blocks):
            for i, v in enumerate(products):
                out_refs[3 * b + i][...] = v[b * rows : (b + 1) * rows].astype(BF16)

    @pl.when(step >= peer_steps)
    def _():
        for b in range(blocks):
            for i, v in enumerate(products):
                cut = slice(i * TILE, (i + 1) * TILE)
                out_refs[3 * b + 2][:, cut] = v[b * rows : (b + 1) * rows]


def project(info, xs, w, pieces=2):
    half, depth = xs[0].shape
    peer_steps = 10 // PER
    steps = 18 // PER
    blocks = pieces // 2
    weights = [
        pl.BlockSpec((depth, TILE), lambda j, s, i=i: (0, s[1 + j * PER + i])) for i in range(PER)
    ]
    rows = 2 * half
    peer = pl.BlockSpec((rows, TILE), lambda j, s: (0, jnp.minimum(j, peer_steps - 1)))
    own = pl.BlockSpec((rows, PER * TILE), lambda j, s: (0, jnp.maximum(j - peer_steps, 0)))
    out = pl.pallas_call(
        lambda *refs: project_kernel(*refs, pieces=pieces, sources=len(xs), blocks=blocks),
        grid_spec=pltpu.PrefetchScalarGridSpec(
            num_scalar_prefetch=1,
            grid=(steps,),
            in_specs=[pl.BlockSpec(memory_space=pl.ANY)] * len(xs) + weights,
            out_specs=[peer, peer, own] * blocks,
            scratch_shapes=[
                pltpu.VMEM((half * pieces, depth), BF16),
                pltpu.SemaphoreType.DMA((pieces,)),
            ],
        ),
        out_shape=[
            sds((rows, 5 * TILE), BF16),
            sds((rows, 5 * TILE), BF16),
            sds((rows, 8 * TILE), F32),
        ]
        * blocks,
        compiler_params=params(),
        cost_estimate=HINT,
        name="project",
    )(info, *xs, *([w] * PER))
    return out


def core_sums(s_ref, own_ref, kv_refs, recv_refs):
    n = recv_refs[0].shape[1]
    first = s_ref[0] == 0
    mine = jnp.where(first, kv_refs[0][...].astype(F32), kv_refs[1][...].astype(F32))
    theirs = jnp.where(first, kv_refs[2][...].astype(F32), kv_refs[3][...].astype(F32))
    halves = [
        own_ref[:, i * n : (i + 1) * n] + r[...].astype(F32) for i, r in enumerate(recv_refs)
    ]
    return halves, mine + theirs


def combine_kernel(s_ref, own_ref, kva_ref, kvb_ref, ra_ref, rb_ref, rka_ref, rkb_ref, o_ref):
    halves, kv = core_sums(s_ref, own_ref, (kva_ref, kvb_ref, rka_ref, rkb_ref), (ra_ref, rb_ref))
    n = ra_ref.shape[1]
    for i, v in enumerate(halves):
        o_ref[:, i * n : (i + 1) * n] = v.astype(BF16)
    o_ref[:, 2 * n :] = kv.astype(BF16)


def sums_specs(rows, n):
    kv = pl.BlockSpec((rows, TILE), lambda i, s: (i, 4))
    half = pl.BlockSpec((rows, n // 2), lambda i, s: (i, s[0]))
    return [pl.BlockSpec((rows, n), lambda i, s: (i, s[0])), kv, kv, half, half, kv, kv]


def combine(chip, own, mine, recv):
    rows = own.shape[0]
    n = own.shape[1] // 2
    part = rows // 2
    other = jnp.reshape(1 - chip, (1,)).astype(jnp.int32)
    return pl.pallas_call(
        combine_kernel,
        grid_spec=pltpu.PrefetchScalarGridSpec(
            num_scalar_prefetch=1,
            grid=(rows // part,),
            in_specs=sums_specs(part, n),
            out_specs=pl.BlockSpec((part, n + TILE), lambda i, s: (i, 0)),
        ),
        out_shape=sds((rows, n + TILE), BF16),
        compiler_params=params(),
        cost_estimate=HINT,
        name="combine",
    )(other, own, *mine, *recv, *recv)


def finish_kernel(s_ref, own_ref, kva_ref, kvb_ref, ra_ref, rb_ref, rka_ref, rkb_ref, *rest):
    x_ref, cos_ref, sin_ref, q_ref, k_ref, v_ref = rest
    halves, kv = core_sums(s_ref, own_ref, (kva_ref, kvb_ref, rka_ref, rkb_ref), (ra_ref, rb_ref))
    n = ra_ref.shape[1]
    cos, sin = cos_ref[...], sin_ref[...]

    def turn(v):
        return v * cos + pltpu.roll(v, HD // 2, 1) * sin

    for i, half in enumerate(halves):
        v = half + x_ref[:, i * n : (i + 1) * n].astype(F32)
        for h in range(n // HD):
            at = i * (n // HD) + h
            q_ref[at] = (turn(v[:, h * HD : (h + 1) * HD]) * QSCALE).astype(BF16)
    kv += x_ref[:, 2 * n :].astype(F32)
    k_ref[...] = turn(kv[:, :HD]).astype(BF16)
    v_ref[...] = kv[:, HD:].astype(BF16)


def finish(chip, own, mine, recv, cross, cos, sin, slot):
    rows = own.shape[0]
    n = own.shape[1] // 2
    part = rows // 2
    here = jnp.reshape(chip, (1,)).astype(jnp.int32)
    row = lambda i, s: (i, 0)
    table = lambda i, s: (slot * (rows // part) + i, 0)
    return pl.pallas_call(
        finish_kernel,
        grid_spec=pltpu.PrefetchScalarGridSpec(
            num_scalar_prefetch=1,
            grid=(rows // part,),
            in_specs=sums_specs(part, n)
            + [
                pl.BlockSpec((part, n + TILE), row),
                pl.BlockSpec((part, HD), table),
                pl.BlockSpec((part, HD), table),
            ],
            out_specs=[
                pl.BlockSpec((n // HD, part, HD), lambda i, s: (0, i, 0)),
                pl.BlockSpec((part, HD), row),
                pl.BlockSpec((part, HD), row),
            ],
        ),
        out_shape=[sds((n // HD, rows, HD), BF16), sds((rows, HD), BF16), sds((rows, HD), BF16)],
        compiler_params=params(),
        cost_estimate=HINT,
        name="finish",
    )(here, own, *mine, *recv, *recv, cross, cos, sin)


KB = 512
CHUNK = 1024
PIECE = 512
LARGE = 2.0**100


def attend_kernel(
    s_ref, q_ref, k_ref, v_ref, ka_ref, kb_ref, va_ref, vb_ref, o_ref, vx_ref, acc_ref, top_ref, at
):
    prefix, live, half = s_ref[at + 2], s_ref[at + 3], s_ref[at + 4]
    rows = ka_ref.shape[0]
    m_rows = q_ref.shape[0]
    span = k_ref.shape[1]
    fresh = 2 * rows
    vx_ref[:span, :HD] = v_ref[0]
    vx_ref[span : span + rows, :HD] = va_ref[...]
    vx_ref[span + rows :, :HD] = vb_ref[...]
    vx_ref[:, HD:] = jnp.ones((span + fresh, HD), BF16)
    nt = (((1,), (1,)), ((), ()))
    count = prefix // KB
    rest = prefix - count * KB

    def product(a, b):
        return lax.dot_general(a, b, nt, preferred_element_type=F32)

    def scores(cut, at):
        return product(q_ref[cut, :], k_ref[0, pl.ds(at, KB), :])

    def fresh_scores(cut):
        row = lax.broadcasted_iota(jnp.int32, (rows, fresh), 0) + half * rows
        place = lax.broadcasted_iota(jnp.int32, (rows, fresh), 1)
        ok = (place <= row) & (place < live)
        q = q_ref[cut, :]
        s = jnp.concatenate([product(q, ka_ref[...]), product(q, kb_ref[...])], 1)
        s = s.reshape(PIECE // rows, rows, fresh)
        return jnp.where(ok[None], s, -1e30).reshape(PIECE, fresh)

    def rest_scores(cut, at):
        place = lax.broadcasted_iota(jnp.int32, (PIECE, KB), 1)
        return jnp.where(place < rest, scores(cut, at), -1e30)

    def add(s, cut, at):
        p = jnp.exp2(s - top_ref[cut, :1]).astype(BF16)
        acc_ref[cut, :] += jnp.dot(p, vx_ref[pl.ds(at, KB), :], preferred_element_type=F32)

    def raise_top(s, cut):
        top_ref[cut, :] = jnp.maximum(top_ref[cut, :], jnp.max(s, axis=1, keepdims=True))

    def block(i):
        return pl.multiple_of(i * KB, KB)

    def cuts(size, visit):
        def step(i, carry):
            visit(pl.ds(pl.multiple_of(i * size, size), size))
            return carry

        lax.fori_loop(0, m_rows // size, step, 0)

    def blocks(stop, visit):
        def step(i, carry):
            visit(block(i))
            return carry

        lax.fori_loop(0, stop, step, 0)

    def sweep():
        acc_ref[...] = jnp.zeros_like(acc_ref)
        cuts(PIECE, lambda cut: add(fresh_scores(cut), cut, span))

        @pl.when(rest > 0)
        def _():
            last = block(count)
            cuts(PIECE, lambda cut: add(rest_scores(cut, last), cut, last))

        cuts(CHUNK, lambda cut: blocks(count, lambda at: add(scores(cut, at), cut, at)))

    top_ref[...] = jnp.full(top_ref.shape, -1e30, F32)
    cuts(PIECE, lambda cut: raise_top(scores(cut, 0), cut))

    def attempt(i):
        @pl.when(i > 0)
        def _():
            cuts(PIECE, lambda cut: raise_top(fresh_scores(cut), cut))
            cuts(PIECE, lambda cut: blocks(count, lambda at: raise_top(scores(cut, at), cut)))

            @pl.when(rest > 0)
            def _():
                last = block(count)
                cuts(PIECE, lambda cut: raise_top(rest_scores(cut, last), cut))

        sweep()
        return jnp.max(jnp.where(acc_ref[:, HD:] < LARGE, 0.0, 1.0))

    def more(state):
        return (state[0] == 0) | ((state[0] == 1) & (state[1] > 0.0))

    lax.while_loop(more, lambda state: (state[0] + 1, attempt(state[0])), (0, 0.0))

    for h in range(m_rows // rows):
        cut = slice(h * rows, (h + 1) * rows)
        o_ref[:, h * HD : (h + 1) * HD] = (acc_ref[cut, :HD] / acc_ref[cut, HD:]).astype(BF16)


def attend(info, slot, q, key_cache, value_cache, ka, kb, va, vb):
    heads, rows, _ = q.shape
    span = key_cache.shape[1]
    m_rows = heads * rows
    at = 5 * slot
    q = q.reshape(m_rows, HD)
    cache = pl.BlockSpec((1, span, HD), lambda i, s: (s[at], 0, s[at + 1]))
    fresh = pl.BlockSpec((rows, HD), whole)
    return pl.pallas_call(
        lambda *refs: attend_kernel(*refs, at=at),
        grid_spec=pltpu.PrefetchScalarGridSpec(
            num_scalar_prefetch=1,
            grid=(1,),
            in_specs=[
                pl.BlockSpec((m_rows, HD), whole),
                cache,
                cache,
                fresh,
                fresh,
                fresh,
                fresh,
            ],
            out_specs=pl.BlockSpec((rows, heads * HD), whole),
            scratch_shapes=[
                pltpu.VMEM((span + 2 * rows, 2 * HD), BF16),
                pltpu.VMEM((m_rows, 2 * HD), F32),
                pltpu.VMEM((m_rows, HD), F32),
            ],
        ),
        out_shape=sds((rows, heads * HD), BF16),
        compiler_params=params(),
        cost_estimate=HINT,
        name="attend",
    )(info, q, key_cache, value_cache, ka, kb, va, vb)


def out_kernel(s_ref, *refs, sources, before, outs):
    a_refs, refs = refs[:sources], refs[sources:]
    x_ref, sem = refs[-2:]
    o_refs = refs[-2 - outs : -2]
    depth = a_refs[0].shape[1]

    @pl.when(pl.program_id(0) == 0)
    def _():
        copies = [
            pltpu.make_async_copy(
                ref, x_ref.at[:, pl.ds(pl.multiple_of(s_ref[i] * depth, depth), depth)], sem.at[i]
            )
            for i, ref in enumerate(a_refs)
        ]
        for c in copies:
            c.start()
        for c in copies:
            c.wait()

    total = jnp.dot(x_ref[...], refs[0][...], preferred_element_type=F32)
    if before:
        total += refs[1][...]
    for i, o_ref in enumerate(o_refs):

        @pl.when(pl.program_id(0) * outs // pl.num_programs(0) == i)
        def _():
            o_ref[...] = total.astype(o_ref.dtype)


def out_project(index, pieces, w, before, first, width, dtype, outs=1, cols=1024):
    rows, depth = pieces[0].shape
    n = len(pieces)
    start = first // cols
    cols = min(cols, width)
    specs = [pl.BlockSpec(memory_space=pl.ANY)] * n + [
        pl.BlockSpec((n * depth, cols), lambda j, s: (s[n], start + j))
    ]
    operands = list(pieces) + [w]
    if before is not None:
        operands.append(before)
        specs.append(pl.BlockSpec((rows, cols), lambda j, s: (0, start + j)))
    each = width // cols // outs
    out = pl.pallas_call(
        lambda *refs: out_kernel(*refs, sources=n, before=before is not None, outs=outs),
        grid_spec=pltpu.PrefetchScalarGridSpec(
            num_scalar_prefetch=1,
            grid=(width // cols,),
            in_specs=specs,
            out_specs=[
                pl.BlockSpec((rows, cols), lambda j, s, i=i: (0, jnp.clip(j - i * each, 0, each - 1)))
                for i in range(outs)
            ],
            scratch_shapes=[pltpu.VMEM((rows, n * depth), BF16), pltpu.SemaphoreType.DMA((n,))],
        ),
        out_shape=[sds((rows, width // outs), dtype)] * outs,
        compiler_params=params(),
        cost_estimate=HINT,
        name="out_project",
    )(index, *operands)
    return out[0] if outs == 1 else out


def choose_kernel(s_ref, a_ref, b_ref, o_ref):
    o_ref[...] = jnp.where(s_ref[0] == 1, a_ref[...], b_ref[...])


def choose(flag, a, b):
    rows, cols = a.shape
    part = rows // 2
    block = pl.BlockSpec((part, cols), lambda i, s: (i, 0))
    return pl.pallas_call(
        choose_kernel,
        grid_spec=pltpu.PrefetchScalarGridSpec(
            num_scalar_prefetch=1,
            grid=(rows // part,),
            in_specs=[block] * 2,
            out_specs=block,
        ),
        out_shape=sds(a.shape, a.dtype),
        compiler_params=params(),
        cost_estimate=HINT,
        name="choose",
    )(flag.astype(jnp.int32)[None], a, b)


def add_kernel(a_ref, b_ref, o_ref):
    o_ref[...] = (a_ref[...].astype(F32) + b_ref[...].astype(F32)).astype(BF16)


def add(a, b, part=0, cuts=1):
    shape = (a.shape[0], a.shape[1] // cuts)
    there = pl.BlockSpec(shape, lambda i: (0, part))
    block = pl.BlockSpec(shape, lambda i: (0, 0))
    return pl.pallas_call(
        add_kernel,
        grid=(1,),
        in_specs=[block if cuts == 1 else there, there],
        out_specs=block,
        out_shape=sds(shape, BF16),
        compiler_params=params(),
        cost_estimate=HINT,
        name="add",
    )(a, b)


def in_turn_kernel(s_ref, ka_ref, kb_ref, va_ref, vb_ref, k0_ref, k1_ref, v0_ref, v1_ref):
    first = s_ref[0] == 1

    @pl.when(first)
    def _():
        k0_ref[...], k1_ref[...] = ka_ref[...], kb_ref[...]
        v0_ref[...], v1_ref[...] = va_ref[...], vb_ref[...]

    @pl.when(jnp.logical_not(first))
    def _():
        k0_ref[...], k1_ref[...] = kb_ref[...], ka_ref[...]
        v0_ref[...], v1_ref[...] = vb_ref[...], va_ref[...]


def in_turn(flag, ka, kb, va, vb):
    block = pl.BlockSpec(ka.shape, whole)
    return pl.pallas_call(
        in_turn_kernel,
        grid_spec=pltpu.PrefetchScalarGridSpec(
            num_scalar_prefetch=1, grid=(1,), in_specs=[block] * 4, out_specs=[block] * 4
        ),
        out_shape=[sds(ka.shape, BF16)] * 4,
        compiler_params=params(),
        cost_estimate=HINT,
        name="in_turn",
    )(flag[None], ka, kb, va, vb)


class Order:
    def __init__(self, mark):
        self.mark = mark

    def wait(self, x):
        x, self.mark = lax.optimization_barrier((x, self.mark))
        return x

    def do(self, f, first, *args):
        return self.wait(f(self.wait(first), *args))


def pipelined_body(
    tokens, norm_gain, qkv_weight, out_weight, key_cache, value_cache, prefix_len, stretch_len
):
    gx = lax.axis_index("gx")
    z = lax.axis_index("gy")
    chip, core = gx // 2, gx % 2
    rows = tokens.shape[0]
    half = rows // 2
    width = out_weight.shape[1]
    pieces = 4
    order = Order(prefix_len)
    do, wait = order.do, order.wait

    def along(x, pairs):
        return lax.ppermute(x, "gy", pairs)

    def over_core(x):
        return lax.ppermute(x, "gx", [(i, i ^ 1) for i in range(4)])

    def over_chip(x):
        return lax.ppermute(x, "gx", [(i, i ^ 2) for i in range(4)])

    sibling = [(0, 1), (1, 0), (2, 3), (3, 2)]
    middle = [(1, 2), (2, 1)]
    outward = [(1, 0), (2, 3)]
    inward = [(0, 1), (3, 2)]
    is_mid = (z == 1) | (z == 2)

    request, second = z // 2, z % 2
    other = 1 - request
    local = jnp.arange(8, dtype=jnp.int32)
    pairs = jnp.array([0, 2, 1, 3, 9, 11, 10, 12], jnp.int32)
    tiles = jnp.concatenate(
        [
            is_mid.astype(jnp.int32)[None],
            pairs + (1 - core) * 4,
            jnp.array([8, 17], jnp.int32),
            (local // 4) * 9 + core * 4 + local % 4,
        ]
    )
    spots = jnp.stack([gx, gx ^ 1, gx ^ 2, gx ^ 3, 0 * gx]).astype(jnp.int32)
    near = jnp.stack([core, 1 - core, chip]).astype(jnp.int32)
    far = jnp.stack([core, 1 - core, 1 - chip]).astype(jnp.int32)

    def pick(flag, a, b):
        return jnp.where(flag, a, b)

    def row_squares(x):
        v = x.astype(F32)
        return jnp.sum(v * v, axis=1, keepdims=True)

    def tables(starts):
        pos = (starts[:, None] + jnp.arange(rows, dtype=jnp.int32)[None, :]).reshape(-1)
        lane = jnp.arange(HD, dtype=jnp.int32)
        freq = THETA ** (-((lane % (HD // 2)).astype(F32) * 2.0) / HD)
        angles = pos.astype(F32)[:, None] * freq[None, :]
        sign = jnp.where(lane < HD // 2, -1.0, 1.0).astype(F32)
        return jnp.cos(angles), jnp.sin(angles) * sign[None, :]

    parts = [(request, second), (request, 1 - second), (other, 0 * z), (other, 0 * z + 1)]

    def numbers(prefix):
        values = [
            v for req, part in parts for v in (req, chip, prefix[req], stretch_len[req], part)
        ]
        return jnp.stack(values).astype(jnp.int32)

    def attention(slot, q, ka, kb, va, vb):
        return attend(info, slot, q, key_cache, value_cache, ka, kb, va, vb)

    at_two = z == 2
    squares = do(row_squares, tokens)
    squares_c = over_core(squares)
    starts = jnp.stack(
        [
            prefix_len[request] + second * rows,
            prefix_len[request] + (1 - second) * rows,
            prefix_len[other],
            prefix_len[other] + rows,
        ]
    )
    squares_c = wait(squares_c)
    squares = do(lambda a: a + squares_c, squares)
    squares_x = wait(over_chip(squares))

    def normed(x, i):
        cut = slice(i * half, (i + 1) * half)
        scale = lax.rsqrt((squares + squares_x)[cut] / D + EPSILON)
        return (x[cut].astype(F32) * scale * norm_gain[None, :]).astype(BF16)

    own_a = do(lambda x: normed(x, 0), tokens)
    a0 = along(own_a, sibling)
    own_b = do(lambda x: normed(x, 1), tokens)
    a1 = along(own_b, sibling)
    *mine_o, keep_o = do(lambda x: project(tiles, [x, own_b], qkv_weight), own_a)
    recv_o = [over_core(x) for x in mine_o]
    a0 = wait(a0)
    m0 = along(do(lambda x: choose(at_two, own_a, x), a0), middle)
    cos, sin = do(tables, starts)
    info = do(numbers, prefix_len)
    recv_o = wait(recv_o)
    cross_o = over_chip(do(lambda x: combine(chip, keep_o, mine_o, x), recv_o))
    a1 = wait(a1)
    m1 = along(do(lambda x: choose(at_two, own_b, x), a1), middle)
    m0 = wait(m0)
    n0 = along(m0, outward)

    *mine_a, keep_a = do(lambda x: project(tiles, [x, a1], qkv_weight), a0)
    recv_a = [over_core(x) for x in mine_a]
    n0 = wait(n0)
    cross_o = wait(cross_o)
    m1 = wait(m1)
    n1 = along(m1, outward)
    m2 = along(do(lambda x: choose(at_two, x, own_a), a0), middle)
    recv_a = wait(recv_a)
    cross_a = over_chip(do(lambda x: combine(chip, keep_a, mine_a, x), recv_a))
    q_o, k_o, v_o = do(
        lambda x: finish(chip, keep_o, mine_o, recv_o, x, cos, sin, 0), cross_o
    )
    n1 = wait(n1)
    cross_a = wait(cross_a)
    q_a, k_a, v_a = do(
        lambda x: finish(chip, keep_a, mine_a, recv_a, x, cos, sin, 1), cross_a
    )
    own_first = (second == 0).astype(jnp.int32)
    k0, k1, v0, v1 = do(lambda k: in_turn(own_first, k_o, k, v_o, v_a), k_a)
    m2 = wait(m2)
    n2 = along(m2, outward)
    m3 = along(do(lambda x: choose(at_two, x, own_b), a1), middle)
    att_a = do(lambda q: attention(1, q, k0, k1, v0, v1), q_a)
    att_ax = over_chip(att_a)
    att_ac = over_core(att_a)
    m3 = wait(m3)
    n3 = along(m3, outward)
    att_o = do(lambda q: attention(0, q, k0, k1, v0, v1), q_o)
    att_ox = over_chip(att_o)
    att_oc = over_core(att_o)
    n2 = wait(n2)
    att_ax = wait(att_ax)
    att_ad = over_core(att_ax)
    att_ac, att_ad = wait((att_ac, att_ad))
    part_a = do(
        lambda a: out_project(
            spots, [a, att_ac, att_ax, att_ad], out_weight, None, 0, width, BF16, 2
        ),
        att_a,
    )
    sum_a = [along(x, inward) for x in part_a]

    att_ox = wait(att_ox)
    att_od = over_core(att_ox)
    n3 = wait(n3)
    out = do(
        lambda x: project(tiles, [x, m1, m2, m3, n0, n1, n2, n3], qkv_weight, 4), m0
    )
    *mine_b, keep_b = out[:3]
    *mine_c, keep_c = out[3:]
    recv_b = [over_core(x) for x in mine_b]
    recv_c = [over_core(x) for x in mine_c]
    att_oc, att_od = wait((att_oc, att_od))
    sum_a[0] = wait(sum_a[0])
    recv_b = wait(recv_b)
    cross_b = over_chip(do(lambda x: combine(chip, keep_b, mine_b, x), recv_b))
    recv_c = wait(recv_c)
    cross_c = over_chip(do(lambda x: combine(chip, keep_c, mine_c, x), recv_c))
    def output_own(i):
        cut = width // 2
        return do(
            lambda a: out_project(
                spots, [a, att_oc, att_ox, att_od], out_weight, None, i * cut, cut, BF16, 2
            ),
            att_o,
        )

    part_o = output_own(0)
    sum_a[1] = wait(sum_a[1])
    cross_b = wait(cross_b)
    q_b, k_b, v_b = do(
        lambda x: finish(chip, keep_b, mine_b, recv_b, x, cos, sin, 2), cross_b
    )
    att_b = do(lambda q: attention(2, q, k_b, k_b, v_b, v_b), q_b)
    att_bx = over_chip(att_b)
    att_bc = over_core(att_b)
    cross_c = wait(cross_c)
    q_c, k_c, v_c = do(
        lambda x: finish(chip, keep_c, mine_c, recv_c, x, cos, sin, 3), cross_c
    )
    att_c = do(lambda q: attention(3, q, k_b, k_c, v_b, v_c), q_c)
    att_cx = over_chip(att_c)
    att_cc = over_core(att_c)
    att_bx = wait(att_bx)
    att_bd = over_core(att_bx)
    att_bc, att_bd = wait((att_bc, att_bd))
    part_b = do(
        lambda a: out_project(
            spots, [a, att_bc, att_bx, att_bd], out_weight, None, 0, width, BF16, 2
        ),
        att_b,
    )
    b1 = [along(x, inward) for x in part_b]
    att_cx = wait(att_cx)
    att_cd = over_core(att_cx)
    att_cc, att_cd = wait((att_cc, att_cd))
    part_c = do(
        lambda a: out_project(
            spots, [a, att_cc, att_cx, att_cd], out_weight, None, 0, width, BF16, 2
        ),
        att_c,
    )
    c1 = [along(x, inward) for x in part_c]
    b2, b3, c2, c3 = [], [], [], []

    def pass_b1(i):
        b1[i // 2] = wait(b1[i // 2])
        b2.append(along(do(add, b1[i // 2], part_b[i // 2], i % 2, 2), middle))

    def pass_b2(i):
        b2[i] = wait(b2[i])
        b3.append(along(do(add, b2[i], part_a[i // 2], i % 2), [(1, 0)]))

    def pass_c1(i):
        c1[i // 2] = wait(c1[i // 2])
        c2.append(along(do(add, c1[i // 2], part_c[i // 2], i % 2, 2), middle))

    def pass_c2(i):
        c2[i] = wait(c2[i])
        c3.append(along(do(add, c2[i], part_a[i // 2], i % 2), [(2, 3)]))

    pass_b1(0)
    pass_b1(1)
    part_o += output_own(1)
    pass_b1(2)
    pass_b1(3)
    pass_b2(0)
    pass_b2(1)
    pass_c1(0)
    pass_c1(1)
    pass_b2(2)
    pass_b2(3)
    pass_c2(0)
    pass_c2(1)
    b3[0] = wait(b3[0])
    b3[1] = wait(b3[1])
    pass_c1(2)
    pass_c1(3)
    b3[2] = wait(b3[2])
    pass_c2(2)
    b3[3] = wait(b3[3])
    pass_c2(3)
    zero = jnp.zeros((), BF16)
    total = lambda *xs: sum(x.astype(F32) for x in xs).astype(BF16)
    side = lambda xs: jnp.concatenate(xs, 1)
    base = do(lambda o: total(side(o), side(sum_a), side(b3), pick(z == 2, side(b2), zero)), part_o)
    c3 = wait(c3)
    ends = (z == 1) & (order.mark[0] > 0)
    return total(base, side(c3), pick(ends, side(c2), zero))


def rotate(values, positions):
    half = values.shape[-1] // 2
    freq = THETA ** (-(jnp.arange(half, dtype=jnp.float32) * 2.0) / values.shape[-1])
    angles = positions.astype(jnp.float32)[:, None] * freq[None, :]
    cosine = jnp.concatenate([jnp.cos(angles), jnp.cos(angles)], -1)[:, None, :]
    sine = jnp.concatenate([jnp.sin(angles), jnp.sin(angles)], -1)[:, None, :]
    turned = jnp.concatenate([-values[..., half:], values[..., :half]], -1)
    return values * cosine + turned * sine


def row_positions(row_ids, prefix_len):
    request = row_ids // STRETCH
    match = request[:, None] == jnp.arange(prefix_len.shape[0], dtype=jnp.int32)[None, :]
    start = jnp.sum(jnp.where(match, prefix_len[None, :], 0), axis=1)
    return start + row_ids % STRETCH


def attend_any(
    queries, offsets, cached_keys, cached_values, fresh_keys, fresh_values, prefix, live
):
    keys = jnp.concatenate([cached_keys, fresh_keys], 0)
    values = jnp.concatenate([cached_values, fresh_values], 0)
    scores = jnp.dot(queries, keys.T, preferred_element_type=jnp.float32) * queries.shape[-1] ** (
        -0.5
    )
    span = cached_keys.shape[0]
    places = jnp.arange(keys.shape[0], dtype=jnp.int32)
    shifted = places - span
    allowed = jnp.where(
        (places < span)[None, :],
        (places < prefix)[None, :],
        (shifted[None, :] < live) & (shifted[None, :] <= offsets[:, None]),
    )
    scores = jnp.where(allowed, scores, -1e30)
    highest = jnp.max(scores, axis=1, keepdims=True)
    weights = jnp.where(allowed, jnp.exp(scores - highest), 0.0)
    total = jnp.sum(weights, axis=1, keepdims=True)
    probs = (weights / total).astype(jnp.bfloat16)
    return jnp.dot(probs, values, preferred_element_type=jnp.float32).astype(jnp.bfloat16)


def general_body(
    tokens, norm_gain, qkv_weight, out_weight, key_cache, value_cache, prefix_len, stretch_len
):
    group = QH // KVH
    index_gx = lax.axis_index("gx")
    whole = lax.all_gather(tokens, "gy", axis=0, tiled=True)
    widened = whole.astype(jnp.float32)
    squares = lax.psum(jnp.sum(widened * widened, axis=1), "gx")
    normed_all = (widened * lax.rsqrt(squares / D + EPSILON)[:, None] * norm_gain[None, :]).astype(
        jnp.bfloat16
    )
    total_rows = normed_all.shape[0]
    local_groups = qkv_weight.shape[1] // ((group + 2) * HD)
    requests = prefix_len.shape[0]
    projected = jnp.dot(normed_all, qkv_weight, preferred_element_type=jnp.float32)
    blocks = projected.reshape(total_rows, local_groups, group + 2, HD)
    query_part = blocks[:, :, :group].reshape(total_rows, local_groups * group * HD)
    pair_part = blocks[:, :, group:].reshape(total_rows, local_groups * 2 * HD)
    query_mine = lax.psum_scatter(query_part, "gx", scatter_dimension=1, tiled=True)
    pair_sums = lax.psum(pair_part, "gx")
    positions = row_positions(jnp.arange(total_rows, dtype=jnp.int32), prefix_len)
    pairs = pair_sums.reshape(total_rows, local_groups, 2, HD)
    fresh_keys = rotate(pairs[:, :, 0], positions).astype(jnp.bfloat16)
    fresh_values = pairs[:, :, 1].astype(jnp.bfloat16)
    heads_here = query_mine.shape[1] // HD
    queries = rotate(query_mine.reshape(total_rows, heads_here, HD), positions).astype(jnp.bfloat16)
    offsets = jnp.arange(STRETCH, dtype=jnp.int32)
    head_columns = []
    for head in range(heads_here):
        group_index = (index_gx * heads_here + head) // group
        request_rows = []
        for request in range(requests):
            lower = request * STRETCH
            upper = lower + STRETCH
            result = attend_any(
                queries[lower:upper, head],
                offsets,
                lax.dynamic_slice_in_dim(key_cache[request], group_index * HD, HD, 1),
                lax.dynamic_slice_in_dim(value_cache[request], group_index * HD, HD, 1),
                lax.dynamic_index_in_dim(fresh_keys[lower:upper], group_index, 1, keepdims=False),
                lax.dynamic_index_in_dim(fresh_values[lower:upper], group_index, 1, keepdims=False),
                prefix_len[request],
                stretch_len[request],
            )
            request_rows.append(result)
        head_columns.append(jnp.concatenate(request_rows, 0))
    local_out = jnp.concatenate(head_columns, 1)
    gathered_out = lax.all_gather(local_out, "gx", axis=1, tiled=True)
    summed = lax.psum_scatter(
        jnp.dot(gathered_out, out_weight, preferred_element_type=jnp.float32),
        "gy",
        scatter_dimension=0,
        tiled=True,
    )
    return summed.astype(jnp.bfloat16)


def solution(mesh):
    placed = (
        P(("groups", "gy"), "gx"),
        P("gx"),
        P("gx", "gy"),
        P("gy", "gx"),
        P("groups", None, "gy"),
        P("groups", None, "gy"),
        P("groups"),
        P("groups"),
    )
    fits = mesh.shape["gx"] == 4 and mesh.shape["gy"] == 4
    return jax.shard_map(
        pipelined_body if fits else general_body,
        mesh=mesh,
        in_specs=placed,
        out_specs=P(("groups", "gy"), "gx"),
        check_vma=False,
    )
```
